512 devices in a mesh: dp: 8 (over z), table: 64 (over x, y, core).
Axes of the slice: x: 4, y: 8, z: 8, core: 2. Of those that a mesh axis runs over, the one named last changes fastest.
Arguments:
- lookups: int32 [524288, 13], P(('dp', 'table')), may hold values from 0 to 2047
- labels: int32 [524288], P(('dp', 'table')), may hold values 0 or 1
- replica: float32 [8, 1024, 128], P('dp'), may hold values from -6 to 6
- hot_state: float32 [8, 1024], P('dp'), may hold values from 0.001 to 0.1
- cold_table: float32 [32768, 128], P('table'), may hold values from -6 to 6
- cold_state: float32 [32768], P('table'), may hold values from 0.001 to 0.1
- w_hidden: bfloat16 [1664, 1024], replicated, may hold values from -0.15625 to 0.15625
- w_head: bfloat16 [1024], replicated, may hold values from -0.1875 to 0.1875
- requests: int32 [8, 64, 64, 16], P(None, 'table'), may hold values from 0 to 511, as said below
- tile_counts: int32 [64, 2], replicated, may hold values from 0 to 2, as said below
- demote_slots: int32 [64, 16], P('table'), may hold values from 0 to 1023, as said below
- demote_rows: int32 [64, 16], P('table'), may hold values from 0 to 511, as said below
- promote_slots: int32 [64, 16], replicated, may hold values from 0 to 1023, as said below
- promote_rows: int32 [64, 16], P('table'), may hold values from 0 to 511, as said below
Outputs:
- logits: float32 [524288], P(('dp', 'table'))
- replica_next: float32 [8, 1024, 128], P('dp')
- hot_state_next: float32 [8, 1024], P('dp')
- cold_next: float32 [32768, 128], P('table')
- cold_state_next: float32 [32768], P('table')
The draws below stay inside these ranges and needn't reach their ends.
Inputs may be any that keep to these rules, and one draw needn't show every extreme that they name: requests[d, t, j, k] is a row local to table device t, never one of t's demote_rows. `tile_counts`: column 0 counts demoted tiles, column 1 promoted tiles; both columns reach 2 on some table device, and column 1 is column 0 reordered over table devices. `demote_slots`: entries i < 8 * tile_counts[t, 0] are live and distinct over all t; later entries are padding and unused. `demote_rows`: live entries as in demote_slots; distinct within a table device. `promote_slots`: entries i < 8 * tile_counts[t, 1] are live; the live promoted slots of all t are exactly the live demoted slots; later entries are padding. `promote_rows`: distinct within a table device and never one of its demote_rows.
All inputs are finite; a program needn't handle non-finite values. No bound on the sum of `labels` on one device may be relied on, other than what follows from the above.
Results may differ from the reference program's by a relative error of at most 0.003.
Values may be sent and summed in bfloat16 or wider, within the bound.
A program may use at most 64 MiB of HBM per device.

```python
import math
import jax
import jax.numpy as jnp
from jax import lax

E = 128
F = 13
HID = 1024
B_DEV = 1024
HOT = 1024
OWN = 512
CAP = 16
TILE = 8
PT_MAX = 2
PCAP = 16
D_IN = 1664
B_TOT = 524288
ROWS_ALL = 32768
N_DP = 8
N_TABLE = 64


def owner_orders(key):
    return jax.vmap(lambda owner_index: jax.random.permutation(jax.random.fold_in(key, 1000 + owner_index), OWN))(jnp.arange(N_TABLE))


def tile_layout(key):
    demote_tiles = jax.random.randint(jax.random.fold_in(key, 2000), (N_TABLE,), 0, PT_MAX + 1)
    fullest = jax.random.randint(jax.random.fold_in(key, 2001), (), 0, N_TABLE)
    demote_tiles = demote_tiles.at[fullest].set(PT_MAX)
    promote_tiles = demote_tiles[jax.random.permutation(jax.random.fold_in(key, 2002), N_TABLE)]
    return (demote_tiles, promote_tiles)


def slot_layout(key):
    demote_tiles, promote_tiles = tile_layout(key)
    slot_order = jax.random.permutation(jax.random.fold_in(key, 2003), HOT)
    moved_rows = jnp.sum(demote_tiles) * TILE
    slot_range = jnp.arange(HOT)
    scores = jax.random.randint(jax.random.fold_in(key, 2004), (HOT,), 0, HOT) * HOT + slot_range
    scores = jnp.where(slot_range < moved_rows, scores, HOT * HOT + slot_range)
    reorder = slot_order[jnp.argsort(scores, stable=True)]
    positions = jnp.arange(PT_MAX * TILE)[None, :]
    demote_start = (jnp.cumsum(demote_tiles) - demote_tiles) * TILE
    promote_start = (jnp.cumsum(promote_tiles) - promote_tiles) * TILE
    demote_at = slot_order[(demote_start[:, None] + positions) % HOT]
    promote_at = reorder[(promote_start[:, None] + positions) % HOT]
    return (demote_at, promote_at)


def draw_requests(key, part):
    orders = owner_orders(key)
    key = jax.random.fold_in(key, 31)
    chosen_rows = jax.random.randint(key, (N_DP, N_TABLE, N_TABLE, CAP), PCAP, OWN)
    owner_axis = jnp.arange(N_TABLE)[None, :, None, None]
    return orders[owner_axis, chosen_rows].astype(jnp.int32)


def draw_tile_counts(key, part):
    demote_tiles, promote_tiles = tile_layout(key)
    return jnp.stack([demote_tiles, promote_tiles], axis=1).astype(jnp.int32)


def draw_demote_slots(key, part):
    demote_at, promote_at = slot_layout(key)
    return demote_at.astype(jnp.int32)


def draw_demote_rows(key, part):
    orders = owner_orders(key)
    return orders[:, :PCAP].astype(jnp.int32)


def draw_promote_slots(key, part):
    demote_at, promote_at = slot_layout(key)
    return promote_at.astype(jnp.int32)


def draw_promote_rows(key, part):
    orders = owner_orders(key)
    return orders[:, PCAP:2 * PCAP].astype(jnp.int32)


def plant(entries, own_key, smallest, top_value):
    dims = entries.shape
    spot = [jax.random.randint(jax.random.fold_in(own_key, axis), (), 0, dims[axis]) for axis in range(len(dims))]
    entries = entries.at[tuple(spot)].set(smallest)
    longest = dims.index(max(dims))
    spot[longest] = (spot[longest] + 1) % dims[longest]
    return entries.at[tuple(spot)].set(top_value)


def level_of(rng, extent, pieces, least, largest):
    factor_of, own = 1.0, jax.random.fold_in(rng, 6)
    for position, blocks in pieces:
        heights = jnp.exp(jax.random.uniform(jax.random.fold_in(own, position), (blocks,), jnp.float32, least / len(pieces), largest / len(pieces)))
        factor_of = factor_of * jnp.repeat(heights, extent[position] // blocks).reshape([-1 if axis == position else 1 for axis in range(len(extent))])
    return factor_of


def scatter_about(stream_key, dims, scale, limit, split=(), held_as=jnp.bfloat16):
    result = jax.random.normal(stream_key, dims, jnp.float32) * scale
    if len(split) > 0:
        result = level_of(stream_key, dims, split, -0.22, 0.18) * result
    return jnp.clip(result, min=-limit, max=limit).astype(held_as)


def setup_inputs(seed: int = 0) -> dict:
    splits = jax.random.split(jax.random.key(seed), 15)
    lookups = plant(jax.random.randint(splits[0], (B_TOT, F), 0, HOT + N_TABLE * CAP), jax.random.fold_in(splits[0], 1), 0, (HOT + N_TABLE * CAP) - 1).astype(jnp.int32)
    labels = plant((jax.random.randint(splits[1], (B_TOT,), 0, 4) < 1).astype(jnp.int32), jax.random.fold_in(splits[1], 1), 0, 1)
    replica = scatter_about(splits[2], (N_DP, HOT, E), 1.0, 6.0, ((0, 8),), jnp.float32)
    hot_state = jnp.clip(jnp.exp(math.log(0.1) - 4.6051702 * jax.random.uniform(splits[3], (N_DP, HOT), jnp.float32) ** level_of(splits[3], (N_DP, HOT), ((0, 8),), -0.2, 0.2)), 0.001, 0.1)
    cold_table = scatter_about(splits[4], (ROWS_ALL, E), 1.0, 6.0, ((0, 64),), jnp.float32)
    cold_state = jnp.clip(jnp.exp(math.log(0.1) - 4.6051702 * jax.random.uniform(splits[5], (ROWS_ALL,), jnp.float32) ** level_of(splits[5], (ROWS_ALL,), ((0, 64),), -0.2, 0.2)), 0.001, 0.1)
    w_hidden = scatter_about(splits[6], (D_IN, HID), D_IN ** -0.5, 0.15625)
    w_head = scatter_about(splits[7], (HID,), HID ** -0.5, 0.1875)
    requests = draw_requests(jax.random.fold_in(splits[14], 71), 0)
    tile_counts = draw_tile_counts(jax.random.fold_in(splits[14], 71), 0)
    demote_slots = draw_demote_slots(jax.random.fold_in(splits[14], 71), 0)
    demote_rows = draw_demote_rows(jax.random.fold_in(splits[14], 71), 0)
    promote_slots = draw_promote_slots(jax.random.fold_in(splits[14], 71), 0)
    promote_rows = draw_promote_rows(jax.random.fold_in(splits[14], 71), 0)
    return {"lookups": lookups, "labels": labels, "replica": replica, "hot_state": hot_state, "cold_table": cold_table, "cold_state": cold_state, "w_hidden": w_hidden, "w_head": w_head, "requests": requests, "tile_counts": tile_counts, "demote_slots": demote_slots, "demote_rows": demote_rows, "promote_slots": promote_slots, "promote_rows": promote_rows}


learn_rate = 0.3

def adagrad(values, accum_state, row_grads):
    renewed = accum_state + lax.optimization_barrier(jnp.mean(row_grads * row_grads, axis=-1))
    return (values - learn_rate * row_grads * lax.rsqrt(renewed)[..., None], renewed)

def dense_pass(embedded, labels, w_hidden, w_head):
    hidden = jnp.dot(embedded, w_hidden, preferred_element_type=jnp.float32)
    sigmoid_hidden = jax.nn.sigmoid(hidden)
    head_float = w_head.astype(jnp.float32)
    logits = lax.optimization_barrier(jnp.sum(hidden * sigmoid_hidden * head_float, axis=1))
    residue = jax.nn.sigmoid(logits) - labels.astype(jnp.float32)
    silu_slope = sigmoid_hidden * (1.0 + hidden * (1.0 - sigmoid_hidden))
    hidden_grad = (residue[:, None] * head_float * silu_slope).astype(jnp.bfloat16)
    input_grad = lax.dot_general(hidden_grad, w_hidden, (((1,), (1,)), ((), ())), preferred_element_type=jnp.float32).astype(jnp.bfloat16)
    return (logits, lax.optimization_barrier(input_grad))

def reference(lookups, labels, replica, hot_state, cold_table, cold_state, w_hidden, w_head, requests, tile_counts, demote_slots, demote_rows, promote_slots, promote_rows):
    per_group = N_TABLE * B_DEV
    all_rows = N_TABLE * OWN
    cold_grad = jnp.zeros((all_rows, E), jnp.float32)
    logit_parts = []
    rows_list = []
    accum_list = []
    device_of = (jnp.arange(per_group, dtype=jnp.int32) // B_DEV)[:, None]
    for data_group in range(N_DP):
        lookup_codes = lookups[data_group * per_group:(data_group + 1) * per_group]
        is_hot = lookup_codes < HOT
        cold_code = jnp.maximum(lookup_codes - HOT, 0)
        owner_of = cold_code // CAP
        slot_of = cold_code % CAP
        local_row = requests[data_group, owner_of, device_of, slot_of]
        global_row = owner_of * OWN + local_row
        hot_vals = replica[data_group][jnp.minimum(lookup_codes, HOT - 1)].astype(jnp.bfloat16)
        cold_vals = cold_table[global_row].astype(jnp.bfloat16)
        embedded = jnp.where(is_hot[..., None], hot_vals, cold_vals).reshape(per_group, F * E)
        logits, input_grad = dense_pass(embedded, labels[data_group * per_group:(data_group + 1) * per_group], w_hidden, w_head)
        logit_parts.append(logits)
        row_grads = input_grad.reshape(-1, E).astype(jnp.float32)
        flat_hot = is_hot.reshape(-1)
        hot_index = jnp.where(flat_hot, lookup_codes.reshape(-1), HOT)
        hot_grad = jax.ops.segment_sum(row_grads, hot_index, num_segments=HOT + 1)[:HOT]
        cold_index = jnp.where(flat_hot, all_rows, global_row.reshape(-1))
        cold_grad = cold_grad + jax.ops.segment_sum(row_grads, cold_index, num_segments=all_rows + 1)[:all_rows]
        rows_new, accum_new = adagrad(replica[data_group], hot_state[data_group], hot_grad)
        rows_list.append(rows_new)
        accum_list.append(accum_new)
    hot_rows = jnp.stack(rows_list)
    hot_accum = jnp.stack(accum_list)
    cold_next, cold_state_next = adagrad(cold_table, cold_state, cold_grad)
    positions = jnp.arange(PCAP, dtype=jnp.int32)[None, :]
    owner_base = (jnp.arange(N_TABLE, dtype=jnp.int32) * OWN)[:, None]
    demote_live = positions < tile_counts[:, 0:1] * TILE
    demote_flat = demote_slots.reshape(-1)
    demote_vals = lax.optimization_barrier(jnp.sum(hot_rows[:, demote_flat], axis=0)) / N_DP
    demote_accum = lax.optimization_barrier(jnp.sum(hot_accum[:, demote_flat], axis=0)) / N_DP
    demote_index = jnp.where(demote_live, owner_base + demote_rows, all_rows).reshape(-1)
    cold_next = cold_next.at[demote_index].set(demote_vals, mode='drop')
    cold_state_next = cold_state_next.at[demote_index].set(demote_accum, mode='drop')
    promote_live = positions < tile_counts[:, 1:2] * TILE
    promote_global = (owner_base + promote_rows).reshape(-1)
    promote_vals = cold_next[promote_global]
    promote_accum = cold_state_next[promote_global]
    slot_index = jnp.where(promote_live, promote_slots, HOT).reshape(-1)
    replica_next = hot_rows.at[:, slot_index].set(promote_vals[None], mode='drop')
    hot_state_next = hot_accum.at[:, slot_index].set(promote_accum[None], mode='drop')
    return (jnp.concatenate(logit_parts), replica_next, hot_state_next, cold_next, cold_state_next)
```

```python
import functools

import jax
import jax.numpy as jnp
from jax import lax
from jax.experimental import pallas as pl
from jax.experimental.pallas import tpu as pltpu
from jax.sharding import PartitionSpec as P

MESH = pl.DeviceIdType.MESH
BF16 = jnp.bfloat16
F32 = jnp.float32
I32 = jnp.int32

TILE = 8
RATE = 0.3
LIMIT = 56 * 1024 * 1024


def vmem():
    return pl.BlockSpec(memory_space=pltpu.VMEM)


def smem():
    return pl.BlockSpec(memory_space=pltpu.SMEM)


def iota(shape, axis):
    return lax.broadcasted_iota(I32, shape, axis)


def ones_where(mask):
    return jnp.where(mask, 1.0, 0.0).astype(BF16)


def dot(a, b):
    return jnp.dot(a, b, preferred_element_type=F32)


def adagrad(values, accum_state, row_grads):
    renewed = accum_state + jnp.mean(row_grads * row_grads, axis=1, keepdims=True)
    return values - RATE * row_grads * lax.rsqrt(renewed), renewed


def column_of(scalars, rows, lanes, dtype):
    row = iota((rows, lanes), 0)
    out = jnp.zeros((rows, lanes), dtype)
    for i in range(rows):
        out = jnp.where(row == i, scalars(i), out)
    return out


def lanes_to_column(row):
    n = row.shape[1]
    return jnp.broadcast_to(row, (8, n)).T[:, :1]


def column_to_lanes(column):
    n = column.shape[0]
    return jnp.broadcast_to(column, (n, 128)).T[:1, :]


def wait_bytes(ref, sem):
    pltpu.make_async_copy(ref, ref, sem).wait()


def greet(axes):
    barrier = pltpu.get_barrier_semaphore()
    total = 0
    for axis in axes:
        n = lax.axis_size(axis)
        me = lax.axis_index(axis)

        def tell(o, carry, axis=axis, n=n, me=me):
            peer = lax.rem(me + o, n)
            pl.semaphore_signal(barrier, inc=1, device_id={axis: peer}, device_id_type=MESH)
            return carry

        lax.fori_loop(1, n, tell, 0)
        total += n - 1
    return barrier, total


def send_blocks(axis, src, dst, rows, per_peer, send_sem, recv_sem):
    n = lax.axis_size(axis)
    me = lax.axis_index(axis)

    def send(o, carry):
        peer = lax.rem(me + o, n)
        start = pl.multiple_of(peer * rows, rows) if per_peer else 0
        pltpu.make_async_remote_copy(
            src_ref=src.at[pl.ds(start, rows)],
            dst_ref=dst.at[pl.ds(pl.multiple_of(me * rows, rows), rows)],
            send_sem=send_sem,
            recv_sem=recv_sem,
            device_id={axis: peer},
            device_id_type=MESH,
        ).start()
        return carry

    lax.fori_loop(1, n, send, 0)


def own_block(axis, src, dst, rows, per_peer):
    me = lax.axis_index(axis)
    here = pl.ds(pl.multiple_of(me * rows, rows), rows)
    dst[here, :] = src[here, :] if per_peer else src[...]


def fetch_kernel(
    promote_rows, cold_state, requests, table, fetched, base, extra, onehot, served, base_own, extra_own, send_sem, recv_sem
):
    n = lax.axis_size("table")
    cap, width = requests.shape[2], table.shape[1]
    own = table.shape[0]
    pad = base_own.shape[0]
    barrier, greeted = greet(("table",))
    wanted = requests[lax.axis_index("dp"), 0]
    lane = iota((cap, own), 1)
    for j in range(n):
        onehot[j * cap : (j + 1) * cap, :] = ones_where(wanted[:, j : j + 1] == lane)
    served[...] = dot(onehot[...], table[...].astype(BF16)).astype(BF16)
    pl.semaphore_wait(barrier, greeted)
    send_blocks("table", served, fetched, cap, True, send_sem.at[0], recv_sem.at[0])
    for i in range(pad):
        base_own[i : i + 1, :] = table[pl.ds(promote_rows[0, i], 1), :]
    state = column_of(lambda i: cold_state[promote_rows[0, i]], pad, width, F32)
    high = state.astype(BF16)
    rest = state - high.astype(F32)
    mid = rest.astype(BF16)
    low = (rest - mid.astype(F32)).astype(BF16)
    place = iota((pad, width), 1)
    parts = jnp.where(place == 0, high.astype(F32), 0.0)
    parts = jnp.where(place == 1, mid.astype(F32), parts)
    parts = jnp.where(place == 2, low.astype(F32), parts)
    extra_own[...] = jnp.where(place == 3, 1.0, parts).astype(BF16)
    send_blocks("table", base_own, base, pad, False, send_sem.at[1], recv_sem.at[1])
    send_blocks("table", extra_own, extra, pad, False, send_sem.at[2], recv_sem.at[2])
    own_block("table", served, fetched, cap, True)
    own_block("table", base_own, base, pad, False)
    own_block("table", extra_own, extra, pad, False)
    got = pl.ds(0, (n - 1) * cap)
    for sem in (send_sem, recv_sem):
        wait_bytes(fetched.at[got], sem.at[0])
        wait_bytes(base.at[got], sem.at[1])
        wait_bytes(extra.at[got], sem.at[2])


def dense_kernel(
    lookups, labels, hot, fetched, w_hidden, w_head, logits, grads, codes, table, embedded, hots, masked, total, logit_column
):
    fields, batch = lookups.shape
    slots, width = hot.shape
    step = 256
    hidden_units = w_hidden.shape[1]
    blocks = slots // step
    for q in range(blocks):
        rows = pl.ds(q * step, step)
        table[:, q * width : (q + 1) * width] = hot[rows, :].astype(BF16)
        table[:, (blocks + q) * width : (blocks + q + 1) * width] = fetched[rows, :]
    padding = jnp.zeros((codes.shape[1] - fields - 1, batch), I32)
    codes[...] = jnp.concatenate([lookups[...], labels[...], padding], axis=0).T
    total[...] = jnp.zeros_like(total)
    span = masked.shape[1] // width
    group = total.shape[0]

    def tile(i, carry):
        rows = pl.ds(pl.multiple_of(i * step, step), step)
        lane = iota((step, step), 1)
        for f in range(fields):
            code = codes[rows, f : f + 1]
            found = dot(ones_where((code & (step - 1)) == lane), table[...])
            block = code // step
            entry = jnp.where(block == 0, found[:, :width], 0.0)
            for q in range(1, 2 * blocks):
                entry = jnp.where(block == q, found[:, q * width : (q + 1) * width], entry)
            embedded[:, f * width : (f + 1) * width] = entry.astype(BF16)
        hidden = dot(embedded[...], w_hidden[...])
        sig = jax.nn.sigmoid(hidden)
        head = w_head[...].astype(F32)
        logit = jnp.sum(hidden * sig * head, axis=1, keepdims=True)
        logit_column[rows, :] = logit
        residue = jax.nn.sigmoid(logit) - codes[rows, fields : fields + 1].astype(F32)
        slope = sig * (1.0 + hidden * (1.0 - sig))
        hidden_grad = (residue * head * slope).astype(BF16)
        input_grad = lax.dot_general(
            hidden_grad, w_hidden[...], (((1,), (1,)), ((), ())), preferred_element_type=F32
        )
        sub = iota((group, step), 0)
        for f in range(fields):
            grad = input_grad[:, f * width : (f + 1) * width].astype(BF16).astype(F32)
            block = codes[rows, f : f + 1] // group
            for q in range(span):
                masked[f * step : (f + 1) * step, q * width : (q + 1) * width] = jnp.where(
                    block == q, grad, 0.0
                ).astype(BF16)
            code = lookups[f : f + 1, rows] & (group - 1)
            hots[:, f * step : (f + 1) * step] = ones_where(code == sub)
        total[...] += dot(hots[...], masked[...])
        return carry

    lax.fori_loop(0, batch // step, tile, 0)
    logits[...] = column_to_lanes(logit_column[...])
    for q in range(span):
        grads[q * group : (q + 1) * group, :] = total[:, q * width : (q + 1) * width].astype(BF16)


def exchange_kernel(
    promote_rows,
    demote_slots,
    hot_state,
    requests,
    grads,
    replica,
    hot_grad,
    promo_grad,
    cold_grad,
    demoted,
    cold_back,
    hot_back,
    local,
    promo_own,
    demote_own,
    hot_own,
    cold_parts,
    promo_parts,
    cold_own,
    promo_sum,
    send_sem,
    recv_sem,
):
    n, groups = lax.axis_size("table"), lax.axis_size("dp")
    slots, width = replica.shape
    own = local.shape[0]
    cap = cold_back.shape[0] // n
    share = own // groups
    pad = promo_own.shape[0]
    barrier, greeted = greet(("table", "dp"))
    pl.semaphore_wait(barrier, greeted)
    hot_part, cold_part = grads.at[pl.ds(0, slots)], grads.at[pl.ds(slots, slots)]
    send_blocks("table", cold_part, cold_back, cap, True, send_sem.at[0], recv_sem.at[0])
    send_blocks("table", hot_part, hot_back, cap, True, send_sem.at[1], recv_sem.at[1])
    own_block("table", cold_part, cold_back, cap, True)
    own_block("table", hot_part, hot_back, cap, True)
    to_rows = ones_where(iota((own, n * cap), 0) == requests[...])
    demote_hot = ones_where(iota((pad, slots), 1) == column_of(lambda i: demote_slots[0, i], pad, slots, I32))
    for i in range(pad):
        demote_own[i : i + 1, :] = replica[pl.ds(demote_slots[0, i], 1), :]
    demote_state = column_of(lambda i: hot_state[0, demote_slots[0, i]], pad, width, F32)
    table_got = pl.ds(0, (n - 1) * cap)
    wait_bytes(cold_back.at[table_got], recv_sem.at[0])
    local[...] = dot(to_rows, cold_back[...])
    for i in range(pad):
        promo_own[i : i + 1, :] = local[pl.ds(promote_rows[0, i], 1), :]
    send_blocks("dp", promo_own, promo_parts, pad, False, send_sem.at[2], recv_sem.at[2])
    send_blocks("dp", local, cold_parts, share, True, send_sem.at[3], recv_sem.at[3])
    own_block("dp", promo_own, promo_parts, pad, False)
    me = lax.axis_index("dp")
    cold_parts[pl.ds(pl.multiple_of(me * share, share), share), :] = local[
        pl.ds(pl.multiple_of(me * share, share), share), :
    ]
    wait_bytes(hot_back.at[table_got], recv_sem.at[1])
    hot_sum = jnp.zeros((cap, width), F32)
    for j in range(n):
        hot_sum += hot_back[j * cap : (j + 1) * cap, :].astype(F32)
    hot_own[...] = hot_sum.astype(BF16)
    send_blocks("table", hot_own, hot_grad, cap, False, send_sem.at[4], recv_sem.at[4])
    own_block("table", hot_own, hot_grad, cap, False)
    wait_bytes(promo_parts.at[pl.ds(0, (groups - 1) * pad)], recv_sem.at[2])
    promo = promo_parts[0:pad, :]
    for g in range(1, groups):
        promo += promo_parts[g * pad : (g + 1) * pad, :]
    promo_sum[...] = promo.astype(BF16)
    send_blocks("table", promo_sum, promo_grad, pad, False, send_sem.at[5], recv_sem.at[5])
    own_block("table", promo_sum, promo_grad, pad, False)
    wait_bytes(cold_parts.at[pl.ds(0, (groups - 1) * share)], recv_sem.at[3])
    cold = cold_parts[0:share, :]
    for g in range(1, groups):
        cold += cold_parts[g * share : (g + 1) * share, :]
    cold_own[...] = cold.astype(BF16)
    send_blocks("dp", cold_own, cold_grad, share, False, send_sem.at[6], recv_sem.at[6])
    own_block("dp", cold_own, cold_grad, share, False)
    wait_bytes(hot_grad.at[table_got], recv_sem.at[4])
    demote_rows, demote_accum = adagrad(demote_own[0:pad, :], demote_state, dot(demote_hot, hot_grad[...]))
    demote_own[0:pad, :] = demote_rows
    demote_own[pad : 2 * pad, :] = demote_accum
    send_blocks("dp", demote_own, demoted, 2 * pad, False, send_sem.at[7], recv_sem.at[7])
    own_block("dp", demote_own, demoted, 2 * pad, False)
    dp_got = groups - 1
    wait_bytes(cold_grad.at[pl.ds(0, dp_got * share)], recv_sem.at[6])
    wait_bytes(promo_grad.at[table_got], recv_sem.at[5])
    wait_bytes(demoted.at[pl.ds(0, dp_got * 2 * pad)], recv_sem.at[7])
    wait_bytes(cold_back.at[table_got], send_sem.at[0])
    wait_bytes(hot_back.at[table_got], send_sem.at[1])
    wait_bytes(promo_parts.at[pl.ds(0, dp_got * pad)], send_sem.at[2])
    wait_bytes(cold_parts.at[pl.ds(0, dp_got * share)], send_sem.at[3])
    wait_bytes(hot_grad.at[table_got], send_sem.at[4])
    wait_bytes(promo_grad.at[table_got], send_sem.at[5])
    wait_bytes(cold_grad.at[pl.ds(0, dp_got * share)], send_sem.at[6])
    wait_bytes(demoted.at[pl.ds(0, dp_got * 2 * pad)], send_sem.at[7])


def update_kernel(
    tile_counts,
    demote_rows,
    promote_lanes,
    hot_grad,
    promo_grad,
    cold_grad,
    demoted,
    base,
    extra,
    replica,
    hot_state,
    table,
    cold_state,
    replica_next,
    hot_state_next,
    cold_next,
    cold_state_next,
    accum,
    *,
    groups,
):
    slots, width = replica.shape
    own = table.shape[0]
    pad = demoted.shape[0] // (2 * groups)
    values, renewed = adagrad(table[...], lanes_to_column(cold_state[...]), cold_grad[...].astype(F32))
    cold_next[...] = values
    accum[...] = jnp.broadcast_to(renewed, (own, width))
    mean = demoted[0 : 2 * pad, :]
    for g in range(1, groups):
        mean += demoted[2 * pad * g : 2 * pad * (g + 1), :]
    mean = mean / groups
    live = tile_counts[lax.axis_index("table"), 0] * TILE
    for i in range(pad):
        @pl.when(i < live)
        def _():
            cold_next[pl.ds(demote_rows[0, i], 1), :] = mean[i : i + 1, :]
            accum[pl.ds(demote_rows[0, i], 1), :] = mean[pad + i : pad + i + 1, :]

    cold_state_next[...] = accum[...].T[:1, :]
    pick = ones_where(iota((slots, promote_lanes.shape[1]), 0) == promote_lanes[...])
    value = base[...]
    high = value.astype(BF16)
    rest = value - high.astype(F32)
    mid = rest.astype(BF16)
    low = (rest - mid.astype(F32)).astype(BF16)
    chosen = dot(pick, jnp.concatenate([high, mid, low, extra[...], promo_grad[...]], axis=1))
    picked_value = (chosen[:, :width] + chosen[:, width : 2 * width]) + chosen[:, 2 * width : 3 * width]
    side = chosen[:, 3 * width : 4 * width]
    picked_state = (side[:, 0:1] + side[:, 1:2]) + side[:, 2:3]
    promoted = side[:, 3:4] > 0.0
    start = jnp.where(promoted, picked_value, replica[...])
    state = jnp.where(promoted, picked_state, lanes_to_column(hot_state[...]))
    grad = jnp.where(promoted, chosen[:, 4 * width :], hot_grad[...].astype(F32))
    values, renewed = adagrad(start, state, grad)
    replica_next[...] = values
    hot_state_next[...] = column_to_lanes(renewed)


def body(
    lookups,
    labels,
    replica,
    hot_state,
    cold_table,
    cold_state,
    w_hidden,
    w_head,
    requests,
    tile_counts,
    demote_slots,
    demote_rows,
    promote_slots,
    promote_rows,
):
    batch, fields = lookups.shape
    slots, width = replica.shape[1:]
    own = cold_table.shape[0]
    groups, n = lax.axis_size("dp"), lax.axis_size("table")
    cap = requests.shape[3]
    pad = demote_slots.shape[1]
    hidden_units = w_hidden.shape[1]
    dma = pltpu.SemaphoreType.DMA
    shape = jax.ShapeDtypeStruct

    fetched, base, extra = pl.pallas_call(
        fetch_kernel,
        out_shape=(
            shape((n * cap, width), BF16),
            shape((n * pad, width), F32),
            shape((n * pad, width), BF16),
        ),
        in_specs=[smem(), smem(), vmem(), vmem()],
        out_specs=(vmem(), vmem(), vmem()),
        scratch_shapes=[
            pltpu.VMEM((n * cap, own), BF16),
            pltpu.VMEM((n * cap, width), BF16),
            pltpu.VMEM((pad, width), F32),
            pltpu.VMEM((pad, width), BF16),
            dma((3,)),
            dma((3,)),
        ],
        compiler_params=pltpu.CompilerParams(collective_id=0, has_side_effects=True, vmem_limit_bytes=LIMIT),
        name="fetch",
    )(promote_rows, cold_state, requests.transpose(0, 1, 3, 2), cold_table)

    logits, grads = pl.pallas_call(
        dense_kernel,
        out_shape=(shape((1, batch), F32), shape((2 * slots, width), BF16)),
        in_specs=[vmem()] * 6,
        out_specs=(vmem(), vmem()),
        scratch_shapes=[
            pltpu.VMEM((batch, 16), I32),
            pltpu.VMEM((256, 8 * width), BF16),
            pltpu.VMEM((256, fields * width), BF16),
            pltpu.VMEM((512, fields * 256), BF16),
            pltpu.VMEM((fields * 256, 4 * width), BF16),
            pltpu.VMEM((512, 4 * width), F32),
            pltpu.VMEM((batch, 1), F32),
        ],
        compiler_params=pltpu.CompilerParams(vmem_limit_bytes=LIMIT),
        name="dense",
    )(
        lookups.T,
        labels.reshape(1, batch),
        replica[0],
        fetched,
        w_hidden,
        w_head.reshape(1, hidden_units),
    )

    wanted = lax.dynamic_index_in_dim(requests, lax.axis_index("dp"), 0, keepdims=False).reshape(1, n * cap)
    hot_grad, promo_grad, cold_grad, demoted = pl.pallas_call(
        exchange_kernel,
        out_shape=(
            shape((slots, width), BF16),
            shape((n * pad, width), BF16),
            shape((own, width), BF16),
            shape((groups * 2 * pad, width), F32),
        ),
        in_specs=[smem(), smem(), smem(), vmem(), vmem(), vmem()],
        out_specs=(vmem(), vmem(), vmem(), vmem()),
        scratch_shapes=[
            pltpu.VMEM((n * cap, width), BF16),
            pltpu.VMEM((slots, width), BF16),
            pltpu.VMEM((own, width), F32),
            pltpu.VMEM((pad, width), F32),
            pltpu.VMEM((2 * pad, width), F32),
            pltpu.VMEM((slots // n, width), BF16),
            pltpu.VMEM((own, width), F32),
            pltpu.VMEM((groups * pad, width), F32),
            pltpu.VMEM((own // groups, width), BF16),
            pltpu.VMEM((pad, width), BF16),
            dma((8,)),
            dma((8,)),
        ],
        compiler_params=pltpu.CompilerParams(collective_id=1, has_side_effects=True, vmem_limit_bytes=LIMIT),
        name="exchange",
    )(promote_rows, demote_slots, hot_state, wanted, grads, replica[0])

    positions = jnp.arange(pad, dtype=I32)
    live = positions[None, :] < tile_counts[:, 1:2] * TILE
    promote_lanes = jnp.where(live, promote_slots, -1).reshape(1, n * pad)
    replica_next, hot_state_next, cold_next, cold_state_next = pl.pallas_call(
        functools.partial(update_kernel, groups=groups),
        out_shape=(
            shape((slots, width), F32),
            shape((1, slots), F32),
            shape((own, width), F32),
            shape((1, own), F32),
        ),
        in_specs=[smem(), smem()] + [vmem()] * 11,
        out_specs=(vmem(), vmem(), vmem(), vmem()),
        scratch_shapes=[pltpu.VMEM((own, width), F32)],
        compiler_params=pltpu.CompilerParams(vmem_limit_bytes=LIMIT),
        name="update",
    )(
        tile_counts,
        demote_rows,
        promote_lanes,
        hot_grad,
        promo_grad,
        cold_grad,
        demoted,
        base,
        extra,
        replica[0],
        hot_state,
        cold_table,
        cold_state.reshape(1, own),
    )
    return (logits[0], replica_next[None], hot_state_next, cold_next, cold_state_next[0])


def solution(mesh):
    return jax.shard_map(
        body,
        mesh=mesh,
        in_specs=(
            P(("dp", "table"), None),
            P(("dp", "table")),
            P("dp", None, None),
            P("dp", None),
            P("table", None),
            P("table"),
            P(),
            P(),
            P(None, "table", None, None),
            P(),
            P("table", None),
            P("table", None),
            P(),
            P("table", None),
        ),
        out_specs=(
            P(("dp", "table")),
            P("dp", None, None),
            P("dp", None),
            P("table", None),
            P("table"),
        ),
        check_vma=False,
    )
```

```python
import functools

import jax
import jax.numpy as jnp
from jax import lax
from jax.experimental import pallas as pl
from jax.experimental.pallas import tpu as pltpu
from jax.sharding import PartitionSpec as P

MESH = pl.DeviceIdType.MESH
BF16 = jnp.bfloat16
F32 = jnp.float32
I32 = jnp.int32

TILE = 8
RATE = 0.3
LIMIT = 56 * 1024 * 1024


def vmem():
    return pl.BlockSpec(memory_space=pltpu.VMEM)


def smem():
    return pl.BlockSpec(memory_space=pltpu.SMEM)


def iota(shape, axis):
    return lax.broadcasted_iota(I32, shape, axis)


def one_hot(codes, shape, axis):
    index = iota(shape, axis).astype(jnp.int16)
    return jnp.where(codes.astype(jnp.int16) == index, jnp.ones(shape, BF16), jnp.zeros(shape, BF16))


def dot(a, b):
    return jnp.dot(a, b, preferred_element_type=F32)


def dot_lanes(a, b):
    return lax.dot_general(a, b, (((1,), (1,)), ((), ())), preferred_element_type=F32)


def split3(value):
    high = value.astype(BF16)
    rest = value - high.astype(F32)
    mid = rest.astype(BF16)
    return high, mid, (rest - mid.astype(F32)).astype(BF16)


def flat_lanes(array):
    n, k = array.shape
    per = 128 // k
    spread = jnp.concatenate([array] * per, axis=1)
    keep = iota((n, 128), 0) % per == iota((n, 128), 1) // k
    rows = jnp.sum(jnp.where(keep, spread, 0.0).reshape(n // per, per, 128), axis=1)
    return jnp.concatenate([rows[i : i + 1, :] for i in range(n // per)], axis=1)


def adagrad(values, accum_state, row_grads):
    renewed = accum_state + jnp.mean(row_grads * row_grads, axis=1, keepdims=True)
    return values - RATE * row_grads * lax.rsqrt(renewed), renewed


def column_of(scalars, rows, lanes, dtype):
    row = iota((rows, lanes), 0)
    out = jnp.zeros((rows, lanes), dtype)
    for i in range(rows):
        out = jnp.where(row == i, scalars(i), out)
    return out


def lanes_to_column(row):
    n = row.shape[1]
    return jnp.broadcast_to(row, (8, n)).T[:, :1]


def column_to_lanes(column):
    n = column.shape[0]
    return jnp.broadcast_to(column, (n, 128)).T[:1, :]


def wait_bytes(ref, sem):
    pltpu.make_async_copy(ref, ref, sem).wait()


def greet(axes):
    barrier = pltpu.get_barrier_semaphore()
    total = 0
    for axis in axes:
        n = lax.axis_size(axis)
        me = lax.axis_index(axis)

        def tell(o, carry, axis=axis, n=n, me=me):
            peer = lax.rem(me + o, n)
            pl.semaphore_signal(barrier, inc=1, device_id={axis: peer}, device_id_type=MESH)
            return carry

        lax.fori_loop(1, n, tell, 0)
        total += n - 1
    return barrier, total


def send_blocks(axis, src, dst, rows, per_peer, send_sem, recv_sem):
    n = lax.axis_size(axis)
    me = lax.axis_index(axis)

    def send(o, carry):
        peer = lax.rem(me + o, n)
        start = pl.multiple_of(peer * rows, rows) if per_peer else 0
        pltpu.make_async_remote_copy(
            src_ref=src.at[pl.ds(start, rows)],
            dst_ref=dst.at[pl.ds(pl.multiple_of(me * rows, rows), rows)],
            send_sem=send_sem,
            recv_sem=recv_sem,
            device_id={axis: peer},
            device_id_type=MESH,
        ).start()
        return carry

    lax.fori_loop(1, n, send, 0)


def own_block(axis, src, dst, rows, per_peer):
    me = lax.axis_index(axis)
    here = pl.ds(pl.multiple_of(me * rows, rows), rows)
    dst[here, :] = src[here, :] if per_peer else src[...]


def step_kernel(
    promote_rows,
    demote_rows,
    demote_slots,
    cold_state_scalars,
    hot_state_scalars,
    lookups,
    labels,
    replica,
    hot_state,
    cold_table,
    cold_state,
    w_hbm,
    w_head,
    requests,
    tile_counts,
    promote_slots,
    logits,
    replica_next,
    hot_state_next,
    cold_next,
    cold_state_next,
    w_hidden,
    w_flipped,
    wanted_rows,
    served,
    fetched,
    base_own,
    base,
    state_own,
    states,
    table,
    rows,
    cold_send,
    hot_send,
    cold_back,
    hot_back,
    local,
    promo_own,
    demote_own,
    hot_own,
    cold_parts,
    promo_parts,
    cold_own,
    promo_sum,
    hot_grad,
    promo_grad,
    cold_grad,
    demoted,
    pick,
    start,
    w_sem,
    send_sem,
    recv_sem,
):
    n, groups = lax.axis_size("table"), lax.axis_size("dp")
    me, group = lax.axis_index("table"), lax.axis_index("dp")
    fields, batch = lookups.shape
    slots, width = replica.shape
    own = cold_table.shape[0]
    cap, pad = requests.shape[2], demote_slots.shape[1]
    share = own // groups
    half = table.shape[1]
    blocks = slots // half
    table_got = pl.ds(0, (n - 1) * cap)
    dp_got = groups - 1

    load = pltpu.make_async_copy(w_hbm, w_hidden, w_sem)
    load.start()
    barrier, greeted = greet(("table", "dp"))

    wanted = requests[group, 0]
    for j in range(n):
        wanted_rows[j * cap : (j + 1) * cap, :] = one_hot(wanted[:, j : j + 1], (cap, own), 1)
    served[...] = dot(wanted_rows[...], cold_table[...].astype(BF16)).astype(BF16)
    pl.semaphore_wait(barrier, greeted)
    send_blocks("table", served, fetched, cap, True, send_sem.at[0], recv_sem.at[0])
    own_block("table", served, fetched, cap, True)

    for q in range(blocks):
        table[q * width : (q + 1) * width, :] = replica[q * half : (q + 1) * half, :].T.astype(BF16)
    for f in range(fields):
        code = lookups[f : f + 1, :]
        found = dot(table[...], one_hot(code & (half - 1), (half, batch), 0))
        block = code >> (half.bit_length() - 1)
        entry = jnp.where(block == 0, found[:width, :], 0.0)
        for q in range(1, blocks):
            entry = jnp.where(block == q, found[q * width : (q + 1) * width, :], entry)
        rows[f * width : (f + 1) * width, :] = entry.astype(BF16)
    load.wait()
    for f in range(fields):
        part = slice(f * width, (f + 1) * width)
        w_flipped[:, part] = w_hidden[part, :].T
    head = jnp.broadcast_to(w_head[...].astype(F32), (width, w_head.shape[1])).T
    for i in range(pad):
        base_own[i : i + 1, :] = cold_table[pl.ds(promote_rows[0, i], 1), :]
    place = iota((8, width), 1)
    state = jnp.zeros((8, width), F32)
    for i in range(pad):
        state = jnp.where(place == i, cold_state_scalars[promote_rows[0, i]], state)
    state_own[...] = state

    wait_bytes(fetched.at[table_got], recv_sem.at[0])
    send_blocks("table", base_own, base, pad, False, send_sem.at[1], recv_sem.at[1])
    send_blocks("table", state_own, states, 8, False, send_sem.at[2], recv_sem.at[2])
    own_block("table", base_own, base, pad, False)
    own_block("table", state_own, states, 8, False)
    for q in range(blocks):
        table[q * width : (q + 1) * width, :] = fetched[q * half : (q + 1) * half, :].astype(F32).T.astype(BF16)
    for f in range(fields):
        code = lookups[f : f + 1, :]
        found = dot(table[...], one_hot(code & (half - 1), (half, batch), 0))
        block = code >> (half.bit_length() - 1)
        entry = rows[f * width : (f + 1) * width, :].astype(F32)
        for q in range(blocks):
            entry = jnp.where(block == blocks + q, found[q * width : (q + 1) * width, :], entry)
        rows[f * width : (f + 1) * width, :] = entry.astype(BF16)

    hidden = dot(w_flipped[...], rows[...])
    sig = jax.nn.sigmoid(hidden)
    heads = jnp.concatenate([head] * (batch // width), axis=1)
    logit = jnp.sum(hidden * sig * heads, axis=0, keepdims=True)
    logits[...] = logit
    residue = jax.nn.sigmoid(logit) - labels[...].astype(F32)
    slope = sig * (1.0 + hidden * (1.0 - sig))
    hidden_grad = (residue * heads * slope).astype(BF16)
    rows[...] = dot(w_hidden[...], hidden_grad).astype(BF16)

    def summed(first, out):
        total = jnp.zeros((half, blocks * width), F32)
        for f in range(fields):
            code = lookups[f : f + 1, :]
            block = code >> (half.bit_length() - 1)
            grad = rows[f * width : (f + 1) * width, :].astype(F32)
            masked = jnp.concatenate(
                [jnp.where(block == first + q, grad, 0.0).astype(BF16) for q in range(blocks)], axis=0
            )
            total += dot_lanes(one_hot(code & (half - 1), (half, batch), 0), masked)
        for q in range(blocks):
            out[q * half : (q + 1) * half, :] = total[:, q * width : (q + 1) * width].astype(BF16)

    summed(blocks, cold_send)
    send_blocks("table", cold_send, cold_back, cap, True, send_sem.at[3], recv_sem.at[3])
    own_block("table", cold_send, cold_back, cap, True)
    summed(0, hot_send)
    send_blocks("table", hot_send, hot_back, cap, True, send_sem.at[4], recv_sem.at[4])
    own_block("table", hot_send, hot_back, cap, True)

    to_rows = one_hot(flat_lanes(wanted.astype(F32).T).astype(I32), (own, n * cap), 0)
    demote_hot = one_hot(column_of(lambda i: demote_slots[0, i], pad, slots, I32), (pad, slots), 1)
    for i in range(pad):
        demote_own[i : i + 1, :] = replica[pl.ds(demote_slots[0, i], 1), :]
    demote_state = column_of(lambda i: hot_state_scalars[0, demote_slots[0, i]], pad, width, F32)
    counts = tile_counts[...]
    live = iota((pad, n), 0) < counts[1:2, :] * TILE
    targets = flat_lanes(jnp.where(live, promote_slots[...], slots).astype(F32).T).astype(I32)
    pick[...] = one_hot(targets, (slots, n * pad), 0)
    wait_bytes(base.at[table_got], recv_sem.at[1])
    wait_bytes(states.at[pl.ds(0, (n - 1) * 8)], recv_sem.at[2])
    chosen = dot(pick[...], jnp.concatenate(split3(base[...]), axis=1))
    picked = (chosen[:, :width] + chosen[:, width : 2 * width]) + chosen[:, 2 * width :]
    state_lanes = flat_lanes(states[...].reshape(n, 8, width)[:, 0, :pad])
    pieces = [piece.astype(F32) for piece in split3(state_lanes)]
    side_rows = jnp.concatenate(pieces + [jnp.ones_like(state_lanes)] + [jnp.zeros_like(state_lanes)] * 4, axis=0)
    side = dot_lanes(pick[...], side_rows.astype(BF16))
    promoted = side[:, 3:4] > 0.0
    start[...] = jnp.where(promoted, picked, replica[...])
    start_state = jnp.where(promoted, (side[:, 0:1] + side[:, 1:2]) + side[:, 2:3], lanes_to_column(hot_state[...]))
    cold_column = lanes_to_column(cold_state[...])

    wait_bytes(cold_back.at[table_got], recv_sem.at[3])
    local[...] = dot(to_rows, cold_back[...])
    for i in range(pad):
        promo_own[i : i + 1, :] = local[pl.ds(promote_rows[0, i], 1), :]
    send_blocks("dp", promo_own, promo_parts, pad, False, send_sem.at[5], recv_sem.at[5])
    send_blocks("dp", local, cold_parts, share, True, send_sem.at[6], recv_sem.at[6])
    own_block("dp", promo_own, promo_parts, pad, False)
    own_block("dp", local, cold_parts, share, True)
    wait_bytes(hot_back.at[table_got], recv_sem.at[4])
    hot_own[...] = jnp.sum(hot_back[...].astype(F32).reshape(n, cap, width), axis=0).astype(BF16)
    send_blocks("table", hot_own, hot_grad, cap, False, send_sem.at[7], recv_sem.at[7])
    own_block("table", hot_own, hot_grad, cap, False)
    wait_bytes(promo_parts.at[pl.ds(0, dp_got * pad)], recv_sem.at[5])
    promo_sum[...] = jnp.sum(promo_parts[...].reshape(groups, pad, width), axis=0).astype(BF16)
    send_blocks("table", promo_sum, promo_grad, pad, False, send_sem.at[8], recv_sem.at[8])
    own_block("table", promo_sum, promo_grad, pad, False)
    wait_bytes(cold_parts.at[pl.ds(0, dp_got * share)], recv_sem.at[6])
    cold_own[...] = jnp.sum(cold_parts[...].reshape(groups, share, width), axis=0).astype(BF16)
    send_blocks("dp", cold_own, cold_grad, share, False, send_sem.at[9], recv_sem.at[9])
    own_block("dp", cold_own, cold_grad, share, False)
    wait_bytes(hot_grad.at[table_got], recv_sem.at[7])
    values, renewed = adagrad(demote_own[0:pad, :], demote_state, dot(demote_hot, hot_grad[...]))
    demote_own[0:pad, :] = values
    demote_own[pad : 2 * pad, :] = renewed
    send_blocks("dp", demote_own, demoted, 2 * pad, False, send_sem.at[10], recv_sem.at[10])
    own_block("dp", demote_own, demoted, 2 * pad, False)
    wait_bytes(cold_grad.at[pl.ds(0, dp_got * share)], recv_sem.at[9])
    values, renewed = adagrad(cold_table[...], cold_column, cold_grad[...].astype(F32))
    wait_bytes(promo_grad.at[table_got], recv_sem.at[8])
    grad = jnp.where(promoted, dot(pick[...], promo_grad[...]), hot_grad[...].astype(F32))
    hot_values, hot_renewed = adagrad(start[...], start_state, grad)
    replica_next[...] = hot_values
    hot_state_next[...] = column_to_lanes(hot_renewed)
    wait_bytes(demoted.at[pl.ds(0, dp_got * 2 * pad)], recv_sem.at[10])
    mean = jnp.sum(demoted[...].reshape(groups, 2 * pad, width), axis=0) / groups
    renewed = jnp.broadcast_to(renewed, (own, width))
    count = jnp.sum(jnp.where(iota((1, n), 1) == me, counts[0:1, :], 0), axis=1, keepdims=True) * TILE
    row = iota((own, width), 0)
    for i in range(pad):
        here = (row == demote_rows[0, i]) & (i < count)
        values = jnp.where(here, mean[i : i + 1, :], values)
        renewed = jnp.where(here, mean[pad + i : pad + i + 1, :], renewed)
    cold_next[...] = values
    cold_state_next[...] = renewed.T[:1, :]

    wait_bytes(fetched.at[table_got], send_sem.at[0])
    wait_bytes(base.at[table_got], send_sem.at[1])
    wait_bytes(states.at[pl.ds(0, (n - 1) * 8)], send_sem.at[2])
    wait_bytes(cold_back.at[table_got], send_sem.at[3])
    wait_bytes(hot_back.at[table_got], send_sem.at[4])
    wait_bytes(promo_parts.at[pl.ds(0, dp_got * pad)], send_sem.at[5])
    wait_bytes(cold_parts.at[pl.ds(0, dp_got * share)], send_sem.at[6])
    wait_bytes(hot_grad.at[table_got], send_sem.at[7])
    wait_bytes(promo_grad.at[table_got], send_sem.at[8])
    wait_bytes(cold_grad.at[pl.ds(0, dp_got * share)], send_sem.at[9])
    wait_bytes(demoted.at[pl.ds(0, dp_got * 2 * pad)], send_sem.at[10])


def body(
    lookups,
    labels,
    replica,
    hot_state,
    cold_table,
    cold_state,
    w_hidden,
    w_head,
    requests,
    tile_counts,
    demote_slots,
    demote_rows,
    promote_slots,
    promote_rows,
):
    batch, fields = lookups.shape
    slots, width = replica.shape[1:]
    own = cold_table.shape[0]
    groups, n = lax.axis_size("dp"), lax.axis_size("table")
    cap = requests.shape[3]
    pad = demote_slots.shape[1]
    inputs, units = w_hidden.shape
    dma = pltpu.SemaphoreType.DMA
    shape = jax.ShapeDtypeStruct
    logits, replica_next, hot_state_next, cold_next, cold_state_next = pl.pallas_call(
        step_kernel,
        out_shape=(
            shape((1, batch), F32),
            shape((slots, width), F32),
            shape((1, slots), F32),
            shape((own, width), F32),
            shape((1, own), F32),
        ),
        in_specs=[smem()] * 5 + [vmem()] * 6 + [pl.BlockSpec(memory_space=pl.ANY)] + [vmem()] * 4,
        out_specs=(vmem(),) * 5,
        scratch_shapes=[
            pltpu.VMEM((inputs, units), BF16),
            pltpu.VMEM((units, inputs), BF16),
            pltpu.VMEM((n * cap, own), BF16),
            pltpu.VMEM((n * cap, width), BF16),
            pltpu.VMEM((n * cap, width), BF16),
            pltpu.VMEM((pad, width), F32),
            pltpu.VMEM((n * pad, width), F32),
            pltpu.VMEM((8, width), F32),
            pltpu.VMEM((n * 8, width), F32),
            pltpu.VMEM((2 * width, 512), BF16),
            pltpu.VMEM((inputs, batch), BF16),
            pltpu.VMEM((n * cap, width), BF16),
            pltpu.VMEM((slots, width), BF16),
            pltpu.VMEM((n * cap, width), BF16),
            pltpu.VMEM((slots, width), BF16),
            pltpu.VMEM((own, width), F32),
            pltpu.VMEM((pad, width), F32),
            pltpu.VMEM((2 * pad, width), F32),
            pltpu.VMEM((slots // n, width), BF16),
            pltpu.VMEM((own, width), F32),
            pltpu.VMEM((groups * pad, width), F32),
            pltpu.VMEM((own // groups, width), BF16),
            pltpu.VMEM((pad, width), BF16),
            pltpu.VMEM((slots, width), BF16),
            pltpu.VMEM((n * pad, width), BF16),
            pltpu.VMEM((own, width), BF16),
            pltpu.VMEM((groups * 2 * pad, width), F32),
            pltpu.VMEM((slots, n * pad), BF16),
            pltpu.VMEM((slots, width), F32),
            dma,
            dma((11,)),
            dma((11,)),
        ],
        compiler_params=pltpu.CompilerParams(collective_id=0, has_side_effects=True, vmem_limit_bytes=LIMIT),
        name="step",
    )(
        promote_rows,
        demote_rows,
        demote_slots,
        cold_state,
        hot_state,
        lookups.T,
        labels.reshape(1, batch),
        replica[0],
        hot_state,
        cold_table,
        cold_state.reshape(1, own),
        w_hidden,
        w_head.reshape(1, units),
        requests.transpose(0, 1, 3, 2),
        tile_counts.T,
        promote_slots.T,
    )
    return (logits[0], replica_next[None], hot_state_next, cold_next, cold_state_next[0])


def solution(mesh):
    return jax.shard_map(
        body,
        mesh=mesh,
        in_specs=(
            P(("dp", "table"), None),
            P(("dp", "table")),
            P("dp", None, None),
            P("dp", None),
            P("table", None),
            P("table"),
            P(),
            P(),
            P(None, "table", None, None),
            P(),
            P("table", None),
            P("table", None),
            P(),
            P("table", None),
        ),
        out_specs=(
            P(("dp", "table")),
            P("dp", None, None),
            P("dp", None),
            P("table", None),
            P("table"),
        ),
        check_vma=False,
    )
```

```python
import functools

import jax
import jax.numpy as jnp
from jax import lax
from jax.experimental import pallas as pl
from jax.experimental.pallas import tpu as pltpu
from jax.sharding import PartitionSpec as P

MESH = pl.DeviceIdType.MESH
BF16 = jnp.bfloat16
F32 = jnp.float32
I32 = jnp.int32

TILE = 8
RATE = 0.3
LIMIT = 56 * 1024 * 1024


def vmem():
    return pl.BlockSpec(memory_space=pltpu.VMEM)


def smem():
    return pl.BlockSpec(memory_space=pltpu.SMEM)


def iota(shape, axis):
    return lax.broadcasted_iota(I32, shape, axis)


def one_hot(codes, shape, axis):
    index = iota(shape, axis).astype(jnp.int16)
    return jnp.where(codes.astype(jnp.int16) == index, jnp.ones(shape, BF16), jnp.zeros(shape, BF16))


def dot(a, b):
    return jnp.dot(a, b, preferred_element_type=F32)


def dot_lanes(a, b):
    return lax.dot_general(a, b, (((1,), (1,)), ((), ())), preferred_element_type=F32)


def split3(value):
    high = value.astype(BF16)
    rest = value - high.astype(F32)
    mid = rest.astype(BF16)
    return high, mid, (rest - mid.astype(F32)).astype(BF16)


def flat_lanes(array):
    n, k = array.shape
    per = 128 // k
    spread = jnp.concatenate([array] * per, axis=1)
    keep = iota((n, 128), 0) % per == iota((n, 128), 1) // k
    rows = jnp.sum(jnp.where(keep, spread, 0.0).reshape(n // per, per, 128), axis=1)
    return jnp.concatenate([rows[i : i + 1, :] for i in range(n // per)], axis=1)


def adagrad(values, accum_state, row_grads):
    renewed = accum_state + jnp.mean(row_grads * row_grads, axis=1, keepdims=True)
    return values - RATE * row_grads * lax.rsqrt(renewed), renewed


def column_of(scalars, rows, lanes, dtype):
    row = iota((rows, lanes), 0)
    out = jnp.zeros((rows, lanes), dtype)
    for i in range(rows):
        out = jnp.where(row == i, scalars(i), out)
    return out


def lanes_to_column(row):
    n = row.shape[1]
    return jnp.broadcast_to(row, (8, n)).T[:, :1]


def column_to_lanes(column):
    n = column.shape[0]
    return jnp.broadcast_to(column, (n, 128)).T[:1, :]


def wait_bytes(ref, sem):
    pltpu.make_async_copy(ref, ref, sem).wait()


def greet(axes):
    barrier = pltpu.get_barrier_semaphore()
    total = 0
    for axis in axes:
        n = lax.axis_size(axis)
        me = lax.axis_index(axis)

        def tell(o, carry, axis=axis, n=n, me=me):
            peer = lax.rem(me + o, n)
            pl.semaphore_signal(barrier, inc=1, device_id={axis: peer}, device_id_type=MESH)
            return carry

        lax.fori_loop(1, n, tell, 0)
        total += n - 1
    return barrier, total


def send_blocks(axis, src, dst, rows, per_peer, send_sem, recv_sem):
    n = lax.axis_size(axis)
    me = lax.axis_index(axis)

    def send(o, carry):
        peer = lax.rem(me + o, n)
        start = pl.multiple_of(peer * rows, rows) if per_peer else 0
        pltpu.make_async_remote_copy(
            src_ref=src.at[pl.ds(start, rows)],
            dst_ref=dst.at[pl.ds(pl.multiple_of(me * rows, rows), rows)],
            send_sem=send_sem,
            recv_sem=recv_sem,
            device_id={axis: peer},
            device_id_type=MESH,
        ).start()
        return carry

    lax.fori_loop(1, n, send, 0)


def own_block(axis, src, dst, rows, per_peer):
    me = lax.axis_index(axis)
    here = pl.ds(pl.multiple_of(me * rows, rows), rows)
    dst[here, :] = src[here, :] if per_peer else src[...]


Y = 8


def remote(src, dst, sems, peer):
    pltpu.make_async_remote_copy(
        src_ref=src, dst_ref=dst, send_sem=sems[0], recv_sem=sems[1], device_id={"table": peer}, device_id_type=MESH
    ).start()


def block_of(index, chips):
    return lax.rem(index, 2) * chips + index // 2


def some_rows(first, count, rows):
    return pl.ds(pl.multiple_of(first * rows, rows), count * rows)


def scatter_by_core(src, dst, rows, sems):
    n = lax.axis_size("table")
    me = lax.axis_index("table")
    here = some_rows(block_of(me, n // 2), 1, rows)

    def send(o, carry):
        peer = lax.rem(me + o, n)
        remote(src.at[some_rows(block_of(peer, n // 2), 1, rows)], dst.at[here], sems, peer)
        return carry

    lax.fori_loop(1, n, send, 0)
    dst[here, :] = src[here, :]


def gather_same_core(src, dst, rows, sems):
    n = lax.axis_size("table")
    me = lax.axis_index("table")
    chips = n // 2
    core, chip = lax.rem(me, 2), me // 2
    here = some_rows(block_of(me, chips), 1, rows)

    def send(o, carry):
        remote(src, dst.at[here], sems, lax.rem(chip + o, chips) * 2 + core)
        return carry

    lax.fori_loop(1, chips, send, 0)
    dst[here, :] = src[...]


def gather_other_core(dst, rows, sems):
    chips = lax.axis_size("table") // 2
    me = lax.axis_index("table")
    core = lax.rem(me, 2)
    half = some_rows(core * chips, chips, rows)
    remote(dst.at[half], dst.at[half], sems, me + 1 - 2 * core)


def gather_along_y(src, dst, rows, sems):
    n = lax.axis_size("table")
    me = lax.axis_index("table")
    core, chip = lax.rem(me, 2), me // 2
    here = some_rows(block_of(me, n // 2), 1, rows)
    for o in range(1, Y):
        peer = (chip // Y * Y + lax.rem(lax.rem(chip, Y) + o, Y)) * 2 + core
        remote(src, dst.at[here], sems, peer)
    dst[here, :] = src[...]


def gather_along_x(dst, rows, sems):
    n = lax.axis_size("table")
    me = lax.axis_index("table")
    chips = n // 2
    core, chip = lax.rem(me, 2), me // 2
    line = some_rows(core * chips + chip // Y * Y, Y, rows)
    for o in range(1, chips // Y):
        remote(dst.at[line], dst.at[line], sems, lax.rem(chip + o * Y, chips) * 2 + core)


def core_major(columns):
    n = columns.shape[1]
    at = iota((n, n), 1)
    order = iota((n, n), 0) == lax.rem(at, n // 2) * 2 + at // (n // 2)
    order = jnp.where(order, 1.0, 0.0).astype(BF16)
    high, low = columns >> 5, columns & 31
    return dot(high.astype(BF16), order) * 32.0 + dot(low.astype(BF16), order)


def step_kernel(
    promote_rows,
    demote_rows,
    demote_slots,
    cold_state_scalars,
    hot_state_scalars,
    lookups,
    labels,
    replica,
    hot_state,
    cold_table,
    cold_state,
    w_hbm,
    w_head,
    requests,
    tile_counts,
    promote_slots,
    logits,
    replica_next,
    hot_state_next,
    cold_next,
    cold_state_next,
    w_hidden,
    w_flipped,
    wanted_rows,
    served,
    fetched,
    base_own,
    base,
    demote_base,
    demote_bases,
    demote_grad,
    demote_grads,
    table,
    rows,
    cold_send,
    hot_send,
    cold_back,
    hot_back,
    local,
    local_send,
    promo_own,
    hot_own,
    cold_parts,
    promo_parts,
    cold_own,
    promo_sum,
    hot_grad,
    promo_grad,
    cold_grad,
    pick,
    start,
    total,
    w_sem,
    send_sem,
    recv_sem,
):
    n, groups = lax.axis_size("table"), lax.axis_size("dp")
    me, group = lax.axis_index("table"), lax.axis_index("dp")
    fields, batch = lookups.shape
    slots, width = replica.shape
    own = cold_table.shape[0]
    cap, pad = requests.shape[2], demote_slots.shape[1]
    share = own // groups
    half = table.shape[1]
    blocks = slots // half
    table_got = pl.ds(0, (n - 1) * cap)
    dp_got = groups - 1
    cells = base_own.shape[0]
    chips = n // 2
    sem = [(send_sem.at[i], recv_sem.at[i]) for i in range(send_sem.shape[0])]

    load = pltpu.make_async_copy(w_hbm, w_hidden, w_sem)
    load.start()
    barrier, greeted = greet(("table", "dp"))

    wanted = requests[group, 0]
    for j in range(n):
        wanted_rows[j * cap : (j + 1) * cap, :] = one_hot(wanted[:, j : j + 1], (cap, own), 1)
    served[...] = dot(wanted_rows[...], cold_table[...].astype(BF16)).astype(BF16)
    pl.semaphore_wait(barrier, greeted)
    send_blocks("table", served, fetched, cap, True, send_sem.at[0], recv_sem.at[0])
    own_block("table", served, fetched, cap, True)
    for i in range(pad):
        demote_base[i : i + 1, :] = replica[pl.ds(demote_slots[0, i], 1), :]
    demote_base[pad : 2 * pad, :] = column_of(lambda i: hot_state_scalars[0, demote_slots[0, i]], pad, width, F32)
    send_blocks("dp", demote_base, demote_bases, 2 * pad, False, send_sem.at[2], recv_sem.at[2])
    own_block("dp", demote_base, demote_bases, 2 * pad, False)

    for q in range(blocks):
        table[q * width : (q + 1) * width, :] = replica[q * half : (q + 1) * half, :].T.astype(BF16)
    def field(f):
        return pl.ds(pl.multiple_of(f * width, width), width)

    def hot_entries(f, carry):
        code = lookups[pl.ds(f, 1), :]
        found = dot(table[...], one_hot(code & (half - 1), (half, batch), 0))
        block = code >> (half.bit_length() - 1)
        entry = jnp.where(block == 0, found[:width, :], 0.0)
        for q in range(1, blocks):
            entry = jnp.where(block == q, found[q * width : (q + 1) * width, :], entry)
        rows[field(f), :] = entry.astype(BF16)
        return carry

    lax.fori_loop(0, fields, hot_entries, 0)
    load.wait()

    def flip(f, carry):
        w_flipped[:, field(f)] = w_hidden[field(f), :].T
        return carry

    lax.fori_loop(0, fields, flip, 0)
    head = jnp.broadcast_to(w_head[...].astype(F32).reshape(1, -1), (width, w_head.shape[0])).T
    for i in range(pad):
        base_own[i : i + 1, :] = cold_table[pl.ds(promote_rows[0, i], 1), :]
    place = iota((8, width), 1)
    state = jnp.zeros((8, width), F32)
    for i in range(pad):
        state = jnp.where(place == i, cold_state_scalars[promote_rows[0, i]], state)
    base_own[pad:cells, :] = state

    wait_bytes(fetched.at[table_got], recv_sem.at[0])
    gather_along_y(base_own, base, cells, sem[1])
    for q in range(blocks):
        table[q * width : (q + 1) * width, :] = fetched[q * half : (q + 1) * half, :].astype(F32).T.astype(BF16)

    def cold_entries(f, carry):
        code = lookups[pl.ds(f, 1), :]
        found = dot(table[...], one_hot(code & (half - 1), (half, batch), 0))
        block = code >> (half.bit_length() - 1)
        entry = rows[field(f), :].astype(F32)
        for q in range(blocks):
            entry = jnp.where(block == blocks + q, found[q * width : (q + 1) * width, :], entry)
        rows[field(f), :] = entry.astype(BF16)
        return carry

    lax.fori_loop(0, fields, cold_entries, 0)

    wait_bytes(base.at[pl.ds(0, (Y - 1) * cells)], recv_sem.at[1])
    gather_along_x(base, cells, sem[11])

    hidden = dot(w_flipped[...], rows[...])
    sig = jax.nn.sigmoid(hidden)
    heads = jnp.concatenate([head] * (batch // width), axis=1)
    logit = jnp.sum(hidden * sig * heads, axis=0, keepdims=True)
    logits[...] = logit
    residue = jax.nn.sigmoid(logit) - labels[...].astype(F32)
    slope = sig * (1.0 + hidden * (1.0 - sig))
    hidden_grad = (residue * heads * slope).astype(BF16)
    rows[...] = dot(w_hidden[...], hidden_grad).astype(BF16)

    def summed(first, out):
        total[...] = jnp.zeros_like(total)

        def add(f, carry):
            code = lookups[pl.ds(f, 1), :]
            block = code >> (half.bit_length() - 1)
            grad = rows[field(f), :].astype(F32)
            masked = jnp.concatenate(
                [jnp.where(block == first + q, grad, 0.0).astype(BF16) for q in range(blocks)], axis=0
            )
            total[...] += dot_lanes(one_hot(code & (half - 1), (half, batch), 0), masked)
            return carry

        lax.fori_loop(0, fields, add, 0)
        for q in range(blocks):
            out[q * half : (q + 1) * half, :] = total[:, q * width : (q + 1) * width].astype(BF16)

    wait_bytes(base.at[pl.ds(0, (chips - Y) * cells)], recv_sem.at[11])
    gather_other_core(base, cells, sem[12])
    summed(blocks, cold_send)
    send_blocks("table", cold_send, cold_back, cap, True, send_sem.at[3], recv_sem.at[3])
    own_block("table", cold_send, cold_back, cap, True)
    summed(0, hot_send)
    scatter_by_core(hot_send, hot_back, cap, sem[4])

    to_rows = one_hot(flat_lanes(wanted.astype(F32).T).astype(I32), (own, n * cap), 0)
    demote_hot = one_hot(column_of(lambda i: demote_slots[0, i], pad, slots, I32), (pad, slots), 1)
    counts = tile_counts[...]
    live = iota((pad, n), 0) < counts[1:2, :] * TILE
    targets = flat_lanes(core_major(jnp.where(live, promote_slots[...], slots)).T).astype(I32)
    pick[...] = one_hot(targets, (slots, n * pad), 0)
    wait_bytes(base.at[pl.ds(0, chips * cells)], recv_sem.at[12])
    bases = base[...].reshape(n, cells, width)
    chosen = dot(pick[...], jnp.concatenate(split3(bases[:, :pad].reshape(n * pad, width)), axis=1))
    picked = (chosen[:, :width] + chosen[:, width : 2 * width]) + chosen[:, 2 * width :]
    state_lanes = flat_lanes(bases[:, pad, :pad])
    pieces = [piece.astype(F32) for piece in split3(state_lanes)]
    side_rows = jnp.concatenate(pieces + [jnp.ones_like(state_lanes)] + [jnp.zeros_like(state_lanes)] * 4, axis=0)
    side = dot_lanes(pick[...], side_rows.astype(BF16))
    promoted = side[:, 3:4] > 0.0
    start[...] = jnp.where(promoted, picked, replica[...])
    start_state = jnp.where(promoted, (side[:, 0:1] + side[:, 1:2]) + side[:, 2:3], lanes_to_column(hot_state[...]))
    cold_column = lanes_to_column(cold_state[...])

    wait_bytes(cold_back.at[table_got], recv_sem.at[3])
    local[...] = dot(to_rows, cold_back[...])
    promo_own[...] = jnp.concatenate([local[pl.ds(promote_rows[0, i], 1), :] for i in range(pad)], axis=0).astype(BF16)
    local_send[...] = local[...].astype(BF16)
    send_blocks("dp", promo_own, promo_parts, pad, False, send_sem.at[5], recv_sem.at[5])
    send_blocks("dp", local_send, cold_parts, share, True, send_sem.at[6], recv_sem.at[6])
    own_block("dp", promo_own, promo_parts, pad, False)
    own_block("dp", local_send, cold_parts, share, True)
    wait_bytes(hot_back.at[table_got], recv_sem.at[4])
    hot_own[...] = jnp.sum(hot_back[...].astype(F32).reshape(n, cap, width), axis=0).astype(BF16)
    gather_same_core(hot_own, hot_grad, cap, sem[7])
    wait_bytes(promo_parts.at[pl.ds(0, dp_got * pad)], recv_sem.at[5])
    promo_sum[...] = jnp.sum(promo_parts[...].astype(F32).reshape(groups, pad, width), axis=0).astype(BF16)
    gather_same_core(promo_sum, promo_grad, pad, sem[8])
    wait_bytes(cold_parts.at[pl.ds(0, dp_got * share)], recv_sem.at[6])
    cold_own[...] = jnp.sum(cold_parts[...].astype(F32).reshape(groups, share, width), axis=0).astype(BF16)
    send_blocks("dp", cold_own, cold_grad, share, False, send_sem.at[9], recv_sem.at[9])
    own_block("dp", cold_own, cold_grad, share, False)
    core_got = pl.ds(0, (chips - 1) * cap)
    half_got = pl.ds(0, chips * cap)
    wait_bytes(hot_grad.at[core_got], recv_sem.at[7])
    gather_other_core(hot_grad, cap, sem[13])
    wait_bytes(hot_grad.at[half_got], recv_sem.at[13])
    demote_grad[...] = dot(demote_hot, hot_grad[...]).astype(BF16)
    send_blocks("dp", demote_grad, demote_grads, pad, False, send_sem.at[10], recv_sem.at[10])
    own_block("dp", demote_grad, demote_grads, pad, False)
    wait_bytes(promo_grad.at[core_got], recv_sem.at[8])
    gather_other_core(promo_grad, pad, sem[14])
    wait_bytes(cold_grad.at[pl.ds(0, dp_got * share)], recv_sem.at[9])
    values, renewed = adagrad(cold_table[...], cold_column, cold_grad[...].astype(F32))
    wait_bytes(promo_grad.at[half_got], recv_sem.at[14])
    grad = jnp.where(promoted, dot(pick[...], promo_grad[...]), hot_grad[...].astype(F32))
    hot_values, hot_renewed = adagrad(start[...], start_state, grad)
    replica_next[...] = hot_values
    hot_state_next[...] = column_to_lanes(hot_renewed)
    wait_bytes(demote_bases.at[pl.ds(0, dp_got * 2 * pad)], recv_sem.at[2])
    wait_bytes(demote_grads.at[pl.ds(0, dp_got * pad)], recv_sem.at[10])
    mean = jnp.zeros((2 * pad, width), F32)
    for g in range(groups):
        old, old_state = demote_bases[2 * pad * g : 2 * pad * g + pad, :], demote_bases[2 * pad * g + pad : 2 * pad * (g + 1), :]
        new, new_state = adagrad(old, old_state, demote_grads[pad * g : pad * (g + 1), :].astype(F32))
        mean += jnp.concatenate([new, new_state], axis=0)
    mean = mean / groups
    renewed = jnp.broadcast_to(renewed, (own, width))
    count = jnp.sum(jnp.where(iota((1, n), 1) == me, counts[0:1, :], 0), axis=1, keepdims=True) * TILE
    row = iota((own, width), 0)
    for i in range(pad):
        here = (row == demote_rows[0, i]) & (i < count)
        values = jnp.where(here, mean[i : i + 1, :], values)
        renewed = jnp.where(here, mean[pad + i : pad + i + 1, :], renewed)
    cold_next[...] = values
    cold_state_next[...] = renewed.T[:1, :]

    for i, sent in enumerate(
        (
            fetched.at[table_got],
            base.at[pl.ds(0, (Y - 1) * cells)],
            demote_bases.at[pl.ds(0, dp_got * 2 * pad)],
            cold_back.at[table_got],
            hot_back.at[table_got],
            promo_parts.at[pl.ds(0, dp_got * pad)],
            cold_parts.at[pl.ds(0, dp_got * share)],
            hot_grad.at[core_got],
            promo_grad.at[core_got],
            cold_grad.at[pl.ds(0, dp_got * share)],
            demote_grads.at[pl.ds(0, dp_got * pad)],
            base.at[pl.ds(0, (chips - Y) * cells)],
            base.at[pl.ds(0, chips * cells)],
            hot_grad.at[half_got],
            promo_grad.at[half_got],
        )
    ):
        wait_bytes(sent, send_sem.at[i])


def finish_kernel(*refs):
    count = len(refs) // 2
    for i in range(count):
        refs[count + i][...] = refs[i][...]


def body(
    lookups,
    labels,
    replica,
    hot_state,
    cold_table,
    cold_state,
    w_hidden,
    w_head,
    requests,
    tile_counts,
    demote_slots,
    demote_rows,
    promote_slots,
    promote_rows,
):
    batch, fields = lookups.shape
    slots, width = replica.shape[1:]
    own = cold_table.shape[0]
    groups, n = lax.axis_size("dp"), lax.axis_size("table")
    cap = requests.shape[3]
    pad = demote_slots.shape[1]
    inputs, units = w_hidden.shape
    dma = pltpu.SemaphoreType.DMA
    shape = jax.ShapeDtypeStruct
    results = (
        shape((1, batch), F32),
        shape((slots, width), F32),
        shape((1, slots), F32),
        shape((own, width), F32),
        shape((1, own), F32),
    )
    found = pl.pallas_call(
        step_kernel,
        out_shape=results,
        in_specs=[smem()] * 5 + [vmem()] * 6 + [pl.BlockSpec(memory_space=pl.ANY)] + [vmem()] * 4,
        out_specs=(vmem(),) * 5,
        scratch_shapes=[
            pltpu.VMEM((inputs, units), BF16),
            pltpu.VMEM((units, inputs), BF16),
            pltpu.VMEM((n * cap, own), BF16),
            pltpu.VMEM((n * cap, width), BF16),
            pltpu.VMEM((n * cap, width), BF16),
            pltpu.VMEM((pad + 8, width), F32),
            pltpu.VMEM((n * (pad + 8), width), F32),
            pltpu.VMEM((2 * pad, width), F32),
            pltpu.VMEM((groups * 2 * pad, width), F32),
            pltpu.VMEM((pad, width), BF16),
            pltpu.VMEM((groups * pad, width), BF16),
            pltpu.VMEM((2 * width, 512), BF16),
            pltpu.VMEM((inputs, batch), BF16),
            pltpu.VMEM((n * cap, width), BF16),
            pltpu.VMEM((slots, width), BF16),
            pltpu.VMEM((n * cap, width), BF16),
            pltpu.VMEM((slots, width), BF16),
            pltpu.VMEM((own, width), F32),
            pltpu.VMEM((own, width), BF16),
            pltpu.VMEM((pad, width), BF16),
            pltpu.VMEM((slots // n, width), BF16),
            pltpu.VMEM((own, width), BF16),
            pltpu.VMEM((groups * pad, width), BF16),
            pltpu.VMEM((own // groups, width), BF16),
            pltpu.VMEM((pad, width), BF16),
            pltpu.VMEM((slots, width), BF16),
            pltpu.VMEM((n * pad, width), BF16),
            pltpu.VMEM((own, width), BF16),
            pltpu.VMEM((slots, n * pad), BF16),
            pltpu.VMEM((slots, width), F32),
            pltpu.VMEM((512, 2 * width), F32),
            dma,
            dma((15,)),
            dma((15,)),
        ],
        compiler_params=pltpu.CompilerParams(collective_id=0, has_side_effects=True, vmem_limit_bytes=LIMIT),
        name="step",
    )(
        promote_rows,
        demote_rows,
        demote_slots,
        cold_state,
        hot_state,
        lookups.T,
        labels.reshape(1, batch),
        replica[0],
        hot_state,
        cold_table,
        cold_state.reshape(1, own),
        w_hidden,
        w_head,
        requests.transpose(0, 1, 3, 2),
        tile_counts.T,
        promote_slots.T,
    )
    logits, replica_next, hot_state_next, cold_next, cold_state_next = pl.pallas_call(
        finish_kernel,
        out_shape=results,
        in_specs=[vmem()] * 5,
        out_specs=[vmem()] * 5,
        compiler_params=pltpu.CompilerParams(vmem_limit_bytes=LIMIT),
        name="finish",
    )(*found)
    return (logits[0], replica_next[None], hot_state_next, cold_next, cold_state_next[0])


def solution(mesh):
    return jax.shard_map(
        body,
        mesh=mesh,
        in_specs=(
            P(("dp", "table"), None),
            P(("dp", "table")),
            P("dp", None, None),
            P("dp", None),
            P("table", None),
            P("table"),
            P(),
            P(),
            P(None, "table", None, None),
            P(),
            P("table", None),
            P("table", None),
            P(),
            P("table", None),
        ),
        out_specs=(
            P(("dp", "table")),
            P("dp", None, None),
            P("dp", None),
            P("table", None),
            P("table"),
        ),
        check_vma=False,
    )
```

```python
import functools

import jax
import jax.numpy as jnp
from jax import lax
from jax.experimental import pallas as pl
from jax.experimental.pallas import tpu as pltpu
from jax.sharding import PartitionSpec as P

MESH = pl.DeviceIdType.MESH
BF16 = jnp.bfloat16
F32 = jnp.float32
I32 = jnp.int32

TILE = 8
RATE = 0.3
GATHER_FIELDS = 2
SUM_FIELDS = 6
LIMIT = 56 * 1024 * 1024


def vmem():
    return pl.BlockSpec(memory_space=pltpu.VMEM)


def smem():
    return pl.BlockSpec(memory_space=pltpu.SMEM)


def iota(shape, axis):
    return lax.broadcasted_iota(I32, shape, axis)


def one_hot(codes, shape, axis):
    index = iota(shape, axis).astype(jnp.int16)
    return jnp.where(codes.astype(jnp.int16) == index, jnp.ones(shape, BF16), jnp.zeros(shape, BF16))


def dot(a, b):
    return jnp.dot(a, b, preferred_element_type=F32)


def dot_lanes(a, b):
    return lax.dot_general(a, b, (((1,), (1,)), ((), ())), preferred_element_type=F32)


def split3(value):
    high = value.astype(BF16)
    rest = value - high.astype(F32)
    mid = rest.astype(BF16)
    return high, mid, (rest - mid.astype(F32)).astype(BF16)


def flat_lanes(array):
    n, k = array.shape
    per = 128 // k
    spread = jnp.concatenate([array] * per, axis=1)
    keep = iota((n, 128), 0) % per == iota((n, 128), 1) // k
    rows = jnp.sum(jnp.where(keep, spread, 0.0).reshape(n // per, per, 128), axis=1)
    return jnp.concatenate([rows[i : i + 1, :] for i in range(n // per)], axis=1)


def adagrad(values, accum_state, row_grads):
    renewed = accum_state + jnp.mean(row_grads * row_grads, axis=1, keepdims=True)
    return values - RATE * row_grads * lax.rsqrt(renewed), renewed


def column_of(scalars, rows, lanes, dtype):
    row = iota((rows, lanes), 0)
    out = jnp.zeros((rows, lanes), dtype)
    for i in range(rows):
        out = jnp.where(row == i, scalars(i), out)
    return out


def lanes_to_column(row):
    n = row.shape[1]
    return jnp.broadcast_to(row, (8, n)).T[:, :1]


def column_to_lanes(column):
    n = column.shape[0]
    return jnp.broadcast_to(column, (n, 128)).T[:1, :]


def wait_bytes(ref, sem):
    pltpu.make_async_copy(ref, ref, sem).wait()


def greet(axes):
    barrier = pltpu.get_barrier_semaphore()
    total = 0
    for axis in axes:
        n = lax.axis_size(axis)
        me = lax.axis_index(axis)

        def tell(o, carry, axis=axis, n=n, me=me):
            peer = lax.rem(me + o, n)
            pl.semaphore_signal(barrier, inc=1, device_id={axis: peer}, device_id_type=MESH)
            return carry

        lax.fori_loop(1, n, tell, 0)
        total += n - 1
    return barrier, total


def send_blocks(axis, src, dst, rows, per_peer, send_sem, recv_sem):
    n = lax.axis_size(axis)
    me = lax.axis_index(axis)

    def send(o, carry):
        peer = lax.rem(me + o, n)
        start = pl.multiple_of(peer * rows, rows) if per_peer else 0
        pltpu.make_async_remote_copy(
            src_ref=src.at[pl.ds(start, rows)],
            dst_ref=dst.at[pl.ds(pl.multiple_of(me * rows, rows), rows)],
            send_sem=send_sem,
            recv_sem=recv_sem,
            device_id={axis: peer},
            device_id_type=MESH,
        ).start()
        return carry

    lax.fori_loop(1, n, send, 0)


def own_block(axis, src, dst, rows, per_peer):
    me = lax.axis_index(axis)
    here = pl.ds(pl.multiple_of(me * rows, rows), rows)
    dst[here, :] = src[here, :] if per_peer else src[...]


Y = 8


def remote(src, dst, sems, peer):
    pltpu.make_async_remote_copy(
        src_ref=src, dst_ref=dst, send_sem=sems[0], recv_sem=sems[1], device_id={"table": peer}, device_id_type=MESH
    ).start()


def block_of(index, chips):
    return lax.rem(index, 2) * chips + index // 2


def some_rows(first, count, rows):
    return pl.ds(pl.multiple_of(first * rows, rows), count * rows)


def scatter_by_core(src, dst, rows, sems):
    n = lax.axis_size("table")
    me = lax.axis_index("table")
    here = some_rows(block_of(me, n // 2), 1, rows)

    def send(o, carry):
        peer = lax.rem(me + o, n)
        remote(src.at[some_rows(block_of(peer, n // 2), 1, rows)], dst.at[here], sems, peer)
        return carry

    lax.fori_loop(1, n, send, 0)
    dst[here, :] = src[here, :]


def gather_same_core(src, dst, rows, sems):
    n = lax.axis_size("table")
    me = lax.axis_index("table")
    chips = n // 2
    core, chip = lax.rem(me, 2), me // 2
    here = some_rows(block_of(me, chips), 1, rows)

    def send(o, carry):
        remote(src, dst.at[here], sems, lax.rem(chip + o, chips) * 2 + core)
        return carry

    lax.fori_loop(1, chips, send, 0)
    dst[here, :] = src[...]


def gather_other_core(dst, rows, sems):
    chips = lax.axis_size("table") // 2
    me = lax.axis_index("table")
    core = lax.rem(me, 2)
    half = some_rows(core * chips, chips, rows)
    remote(dst.at[half], dst.at[half], sems, me + 1 - 2 * core)


def gather_along_y(src, dst, rows, sems):
    n = lax.axis_size("table")
    me = lax.axis_index("table")
    core, chip = lax.rem(me, 2), me // 2
    here = some_rows(block_of(me, n // 2), 1, rows)
    for o in range(1, Y):
        peer = (chip // Y * Y + lax.rem(lax.rem(chip, Y) + o, Y)) * 2 + core
        remote(src, dst.at[here], sems, peer)
    dst[here, :] = src[...]


def gather_along_x(dst, rows, sems):
    n = lax.axis_size("table")
    me = lax.axis_index("table")
    chips = n // 2
    core, chip = lax.rem(me, 2), me // 2
    line = some_rows(core * chips + chip // Y * Y, Y, rows)
    for o in range(1, chips // Y):
        remote(dst.at[line], dst.at[line], sems, lax.rem(chip + o * Y, chips) * 2 + core)


def core_major(columns):
    n = columns.shape[1]
    at = iota((n, n), 1)
    order = iota((n, n), 0) == lax.rem(at, n // 2) * 2 + at // (n // 2)
    order = jnp.where(order, 1.0, 0.0).astype(BF16)
    high, low = columns >> 5, columns & 31
    return dot(high.astype(BF16), order) * 32.0 + dot(low.astype(BF16), order)


def step_kernel(
    promote_rows,
    demote_rows,
    demote_slots,
    cold_state_scalars,
    hot_state_scalars,
    lookups,
    labels,
    replica,
    hot_state,
    cold_table,
    cold_state,
    w_hbm,
    w_head,
    requests,
    tile_counts,
    promote_slots,
    logits,
    replica_next,
    hot_state_next,
    cold_next,
    cold_state_next,
    w_hidden,
    w_flipped,
    wanted_rows,
    served,
    fetched,
    base_own,
    base,
    demote_base,
    demote_bases,
    demote_grad,
    demote_grads,
    table,
    rows,
    cold_send,
    hot_send,
    cold_back,
    hot_back,
    local,
    local_send,
    promo_own,
    hot_own,
    cold_parts,
    promo_parts,
    cold_own,
    promo_sum,
    hot_grad,
    promo_grad,
    cold_grad,
    pick,
    start,
    total,
    w_sem,
    send_sem,
    recv_sem,
):
    n, groups = lax.axis_size("table"), lax.axis_size("dp")
    me, group = lax.axis_index("table"), lax.axis_index("dp")
    fields, batch = lookups.shape
    slots, width = replica.shape
    own = cold_table.shape[0]
    cap, pad = requests.shape[2], demote_slots.shape[1]
    share = own // groups
    half = table.shape[1]
    blocks = slots // half
    table_got = pl.ds(0, (n - 1) * cap)
    dp_got = groups - 1
    cells = base_own.shape[0]
    chips = n // 2
    sem = [(send_sem.at[i], recv_sem.at[i]) for i in range(send_sem.shape[0])]

    load = pltpu.make_async_copy(w_hbm, w_hidden, w_sem)
    load.start()
    barrier, greeted = greet(("table", "dp"))

    wanted = requests[group, 0]
    for j in range(n):
        wanted_rows[j * cap : (j + 1) * cap, :] = one_hot(wanted[:, j : j + 1], (cap, own), 1)
    served[...] = dot(wanted_rows[...], cold_table[...].astype(BF16)).astype(BF16)
    pl.semaphore_wait(barrier, greeted)
    send_blocks("table", served, fetched, cap, True, send_sem.at[0], recv_sem.at[0])
    own_block("table", served, fetched, cap, True)
    for i in range(pad):
        demote_base[i : i + 1, :] = replica[pl.ds(demote_slots[0, i], 1), :]
    demote_base[pad : 2 * pad, :] = column_of(lambda i: hot_state_scalars[0, demote_slots[0, i]], pad, width, F32)
    send_blocks("dp", demote_base, demote_bases, 2 * pad, False, send_sem.at[2], recv_sem.at[2])
    own_block("dp", demote_base, demote_bases, 2 * pad, False)

    for q in range(blocks):
        table[q * width : (q + 1) * width, :] = replica[q * half : (q + 1) * half, :].T.astype(BF16)
    def field(f):
        return pl.ds(pl.multiple_of(f * width, width), width)

    def by_fields(count, step):
        def some(k, carry):
            step([k * count + i for i in range(count)])
            return carry

        lax.fori_loop(0, fields // count, some, 0)
        if fields % count:
            step(list(range(fields - fields % count, fields)))

    def hot_entry(f):
        code = lookups[pl.ds(f, 1), :]
        found = dot(table[...], one_hot(code & (half - 1), (half, batch), 0))
        block = code >> (half.bit_length() - 1)
        entry = jnp.where(block == 0, found[:width, :], 0.0)
        for q in range(1, blocks):
            entry = jnp.where(block == q, found[q * width : (q + 1) * width, :], entry)
        rows[field(f), :] = entry.astype(BF16)

    by_fields(GATHER_FIELDS, lambda some: [hot_entry(f) for f in some])
    load.wait()

    def flip(f, carry):
        w_flipped[:, field(f)] = w_hidden[field(f), :].T
        return carry

    lax.fori_loop(0, fields, flip, 0)
    head = jnp.broadcast_to(w_head[...].astype(F32).reshape(1, -1), (width, w_head.shape[0])).T
    for i in range(pad):
        base_own[i : i + 1, :] = cold_table[pl.ds(promote_rows[0, i], 1), :]
    place = iota((8, width), 1)
    state = jnp.zeros((8, width), F32)
    for i in range(pad):
        state = jnp.where(place == i, cold_state_scalars[promote_rows[0, i]], state)
    base_own[pad:cells, :] = state

    wait_bytes(fetched.at[table_got], recv_sem.at[0])
    gather_along_y(base_own, base, cells, sem[1])
    for q in range(blocks):
        table[q * width : (q + 1) * width, :] = fetched[q * half : (q + 1) * half, :].astype(F32).T.astype(BF16)

    def cold_entry(f):
        code = lookups[pl.ds(f, 1), :]
        found = dot(table[...], one_hot(code & (half - 1), (half, batch), 0))
        block = code >> (half.bit_length() - 1)
        entry = rows[field(f), :].astype(F32)
        for q in range(blocks):
            entry = jnp.where(block == blocks + q, found[q * width : (q + 1) * width, :], entry)
        rows[field(f), :] = entry.astype(BF16)

    by_fields(GATHER_FIELDS, lambda some: [cold_entry(f) for f in some])

    wait_bytes(base.at[pl.ds(0, (Y - 1) * cells)], recv_sem.at[1])
    gather_along_x(base, cells, sem[11])

    hidden = dot(w_flipped[...], rows[...])
    sig = jax.nn.sigmoid(hidden)
    heads = jnp.concatenate([head] * (batch // width), axis=1)
    logit = jnp.sum(hidden * sig * heads, axis=0, keepdims=True)
    logits[...] = logit
    residue = jax.nn.sigmoid(logit) - labels[...].astype(F32)
    slope = sig * (1.0 + hidden * (1.0 - sig))
    hidden_grad = (residue * heads * slope).astype(BF16)
    rows[...] = dot(w_hidden[...], hidden_grad).astype(BF16)

    def summed(first, out):
        total[...] = jnp.zeros_like(total)

        def add(some):
            picks, grads = [], []
            for f in some:
                code = lookups[pl.ds(f, 1), :]
                block = code >> (half.bit_length() - 1)
                grad = rows[field(f), :]
                keep = [jnp.where(block == first + q, 1.0, 0.0).astype(BF16) for q in range(blocks)]
                grads.append(jnp.concatenate([grad * mask for mask in keep], axis=0))
                picks.append(one_hot(code & (half - 1), (half, batch), 0))
            total[...] += dot_lanes(jnp.concatenate(picks, axis=1), jnp.concatenate(grads, axis=1))

        by_fields(SUM_FIELDS, add)
        for q in range(blocks):
            out[q * half : (q + 1) * half, :] = total[:, q * width : (q + 1) * width].astype(BF16)

    wait_bytes(base.at[pl.ds(0, (chips - Y) * cells)], recv_sem.at[11])
    gather_other_core(base, cells, sem[12])
    summed(blocks, cold_send)
    send_blocks("table", cold_send, cold_back, cap, True, send_sem.at[3], recv_sem.at[3])
    own_block("table", cold_send, cold_back, cap, True)
    summed(0, hot_send)
    scatter_by_core(hot_send, hot_back, cap, sem[4])

    to_rows = one_hot(flat_lanes(wanted.astype(F32).T).astype(I32), (own, n * cap), 0)
    demote_hot = one_hot(column_of(lambda i: demote_slots[0, i], pad, slots, I32), (pad, slots), 1)
    counts = tile_counts[...]
    live = iota((pad, n), 0) < counts[1:2, :] * TILE
    targets = flat_lanes(core_major(jnp.where(live, promote_slots[...], slots)).T).astype(I32)
    pick[...] = one_hot(targets, (slots, n * pad), 0)

    wait_bytes(cold_back.at[table_got], recv_sem.at[3])
    local[...] = dot(to_rows, cold_back[...])
    promo_own[...] = jnp.concatenate([local[pl.ds(promote_rows[0, i], 1), :] for i in range(pad)], axis=0).astype(BF16)
    local_send[...] = local[...].astype(BF16)
    send_blocks("dp", promo_own, promo_parts, pad, False, send_sem.at[5], recv_sem.at[5])
    send_blocks("dp", local_send, cold_parts, share, True, send_sem.at[6], recv_sem.at[6])
    own_block("dp", promo_own, promo_parts, pad, False)
    own_block("dp", local_send, cold_parts, share, True)
    wait_bytes(hot_back.at[table_got], recv_sem.at[4])
    hot_own[...] = jnp.sum(hot_back[...].astype(F32).reshape(n, cap, width), axis=0).astype(BF16)
    gather_same_core(hot_own, hot_grad, cap, sem[7])
    wait_bytes(promo_parts.at[pl.ds(0, dp_got * pad)], recv_sem.at[5])
    promo_sum[...] = jnp.sum(promo_parts[...].astype(F32).reshape(groups, pad, width), axis=0).astype(BF16)
    gather_same_core(promo_sum, promo_grad, pad, sem[8])
    wait_bytes(cold_parts.at[pl.ds(0, dp_got * share)], recv_sem.at[6])
    cold_own[...] = jnp.sum(cold_parts[...].astype(F32).reshape(groups, share, width), axis=0).astype(BF16)
    send_blocks("dp", cold_own, cold_grad, share, False, send_sem.at[9], recv_sem.at[9])
    own_block("dp", cold_own, cold_grad, share, False)
    wait_bytes(base.at[pl.ds(0, chips * cells)], recv_sem.at[12])
    bases = base[...].reshape(n, cells, width)
    chosen = dot(pick[...], jnp.concatenate(split3(bases[:, :pad].reshape(n * pad, width)), axis=1))
    picked = (chosen[:, :width] + chosen[:, width : 2 * width]) + chosen[:, 2 * width :]
    state_lanes = flat_lanes(bases[:, pad, :pad])
    pieces = [piece.astype(F32) for piece in split3(state_lanes)]
    side_rows = jnp.concatenate(pieces + [jnp.ones_like(state_lanes)] + [jnp.zeros_like(state_lanes)] * 4, axis=0)
    side = dot_lanes(pick[...], side_rows.astype(BF16))
    promoted = side[:, 3:4] > 0.0
    start[...] = jnp.where(promoted, picked, replica[...])
    start_state = jnp.where(promoted, (side[:, 0:1] + side[:, 1:2]) + side[:, 2:3], lanes_to_column(hot_state[...]))
    cold_column = lanes_to_column(cold_state[...])
    core_got = pl.ds(0, (chips - 1) * cap)
    half_got = pl.ds(0, chips * cap)
    wait_bytes(hot_grad.at[core_got], recv_sem.at[7])
    gather_other_core(hot_grad, cap, sem[13])
    wait_bytes(hot_grad.at[half_got], recv_sem.at[13])
    demote_grad[...] = dot(demote_hot, hot_grad[...]).astype(BF16)
    send_blocks("dp", demote_grad, demote_grads, pad, False, send_sem.at[10], recv_sem.at[10])
    own_block("dp", demote_grad, demote_grads, pad, False)
    wait_bytes(promo_grad.at[core_got], recv_sem.at[8])
    gather_other_core(promo_grad, pad, sem[14])
    wait_bytes(cold_grad.at[pl.ds(0, dp_got * share)], recv_sem.at[9])
    values, renewed = adagrad(cold_table[...], cold_column, cold_grad[...].astype(F32))
    wait_bytes(promo_grad.at[half_got], recv_sem.at[14])
    grad = jnp.where(promoted, dot(pick[...], promo_grad[...]), hot_grad[...].astype(F32))
    hot_values, hot_renewed = adagrad(start[...], start_state, grad)
    replica_next[...] = hot_values
    hot_state_next[...] = column_to_lanes(hot_renewed)
    wait_bytes(demote_bases.at[pl.ds(0, dp_got * 2 * pad)], recv_sem.at[2])
    wait_bytes(demote_grads.at[pl.ds(0, dp_got * pad)], recv_sem.at[10])
    mean = jnp.zeros((2 * pad, width), F32)
    for g in range(groups):
        old, old_state = demote_bases[2 * pad * g : 2 * pad * g + pad, :], demote_bases[2 * pad * g + pad : 2 * pad * (g + 1), :]
        new, new_state = adagrad(old, old_state, demote_grads[pad * g : pad * (g + 1), :].astype(F32))
        mean += jnp.concatenate([new, new_state], axis=0)
    mean = mean / groups
    renewed = jnp.broadcast_to(renewed, (own, width))
    count = jnp.sum(jnp.where(iota((1, n), 1) == me, counts[0:1, :], 0), axis=1, keepdims=True) * TILE
    row = iota((own, width), 0)
    for i in range(pad):
        here = (row == demote_rows[0, i]) & (i < count)
        values = jnp.where(here, mean[i : i + 1, :], values)
        renewed = jnp.where(here, mean[pad + i : pad + i + 1, :], renewed)
    cold_next[...] = values
    cold_state_next[...] = renewed.T[:1, :]

    for i, sent in enumerate(
        (
            fetched.at[table_got],
            base.at[pl.ds(0, (Y - 1) * cells)],
            demote_bases.at[pl.ds(0, dp_got * 2 * pad)],
            cold_back.at[table_got],
            hot_back.at[table_got],
            promo_parts.at[pl.ds(0, dp_got * pad)],
            cold_parts.at[pl.ds(0, dp_got * share)],
            hot_grad.at[core_got],
            promo_grad.at[core_got],
            cold_grad.at[pl.ds(0, dp_got * share)],
            demote_grads.at[pl.ds(0, dp_got * pad)],
            base.at[pl.ds(0, (chips - Y) * cells)],
            base.at[pl.ds(0, chips * cells)],
            hot_grad.at[half_got],
            promo_grad.at[half_got],
        )
    ):
        wait_bytes(sent, send_sem.at[i])


def finish_kernel(*refs):
    count = len(refs) // 2
    for i in range(count):
        refs[count + i][...] = refs[i][...]


def body(
    lookups,
    labels,
    replica,
    hot_state,
    cold_table,
    cold_state,
    w_hidden,
    w_head,
    requests,
    tile_counts,
    demote_slots,
    demote_rows,
    promote_slots,
    promote_rows,
):
    batch, fields = lookups.shape
    slots, width = replica.shape[1:]
    own = cold_table.shape[0]
    groups, n = lax.axis_size("dp"), lax.axis_size("table")
    cap = requests.shape[3]
    pad = demote_slots.shape[1]
    inputs, units = w_hidden.shape
    dma = pltpu.SemaphoreType.DMA
    shape = jax.ShapeDtypeStruct
    results = (
        shape((1, batch), F32),
        shape((slots, width), F32),
        shape((1, slots), F32),
        shape((own, width), F32),
        shape((1, own), F32),
    )
    found = pl.pallas_call(
        step_kernel,
        out_shape=results,
        in_specs=[smem()] * 5 + [vmem()] * 6 + [pl.BlockSpec(memory_space=pl.ANY)] + [vmem()] * 4,
        out_specs=(vmem(),) * 5,
        scratch_shapes=[
            pltpu.VMEM((inputs, units), BF16),
            pltpu.VMEM((units, inputs), BF16),
            pltpu.VMEM((n * cap, own), BF16),
            pltpu.VMEM((n * cap, width), BF16),
            pltpu.VMEM((n * cap, width), BF16),
            pltpu.VMEM((pad + 8, width), F32),
            pltpu.VMEM((n * (pad + 8), width), F32),
            pltpu.VMEM((2 * pad, width), F32),
            pltpu.VMEM((groups * 2 * pad, width), F32),
            pltpu.VMEM((pad, width), BF16),
            pltpu.VMEM((groups * pad, width), BF16),
            pltpu.VMEM((2 * width, 512), BF16),
            pltpu.VMEM((inputs, batch), BF16),
            pltpu.VMEM((n * cap, width), BF16),
            pltpu.VMEM((slots, width), BF16),
            pltpu.VMEM((n * cap, width), BF16),
            pltpu.VMEM((slots, width), BF16),
            pltpu.VMEM((own, width), F32),
            pltpu.VMEM((own, width), BF16),
            pltpu.VMEM((pad, width), BF16),
            pltpu.VMEM((slots // n, width), BF16),
            pltpu.VMEM((own, width), BF16),
            pltpu.VMEM((groups * pad, width), BF16),
            pltpu.VMEM((own // groups, width), BF16),
            pltpu.VMEM((pad, width), BF16),
            pltpu.VMEM((slots, width), BF16),
            pltpu.VMEM((n * pad, width), BF16),
            pltpu.VMEM((own, width), BF16),
            pltpu.VMEM((slots, n * pad), BF16),
            pltpu.VMEM((slots, width), F32),
            pltpu.VMEM((512, 2 * width), F32),
            dma,
            dma((15,)),
            dma((15,)),
        ],
        compiler_params=pltpu.CompilerParams(collective_id=0, has_side_effects=True, vmem_limit_bytes=LIMIT),
        name="step",
    )(
        promote_rows,
        demote_rows,
        demote_slots,
        cold_state,
        hot_state,
        lookups.T,
        labels.reshape(1, batch),
        replica[0],
        hot_state,
        cold_table,
        cold_state.reshape(1, own),
        w_hidden,
        w_head,
        requests.transpose(0, 1, 3, 2),
        tile_counts.T,
        promote_slots.T,
    )
    logits, replica_next, hot_state_next, cold_next, cold_state_next = pl.pallas_call(
        finish_kernel,
        out_shape=results,
        in_specs=[vmem()] * 5,
        out_specs=[vmem()] * 5,
        compiler_params=pltpu.CompilerParams(vmem_limit_bytes=LIMIT),
        name="finish",
    )(*found)
    return (logits[0], replica_next[None], hot_state_next, cold_next, cold_state_next[0])


def solution(mesh):
    return jax.shard_map(
        body,
        mesh=mesh,
        in_specs=(
            P(("dp", "table"), None),
            P(("dp", "table")),
            P("dp", None, None),
            P("dp", None),
            P("table", None),
            P("table"),
            P(),
            P(),
            P(None, "table", None, None),
            P(),
            P("table", None),
            P("table", None),
            P(),
            P("table", None),
        ),
        out_specs=(
            P(("dp", "table")),
            P("dp", None, None),
            P("dp", None),
            P("table", None),
            P("table"),
        ),
        check_vma=False,
    )
```

```python
import functools

import jax
import jax.numpy as jnp
from jax import lax
from jax.experimental import pallas as pl
from jax.experimental.pallas import tpu as pltpu
from jax.sharding import PartitionSpec as P

MESH = pl.DeviceIdType.MESH
BF16 = jnp.bfloat16
F32 = jnp.float32
I32 = jnp.int32

TILE = 8
RATE = 0.3
GATHER_FIELDS = 2
SUM_FIELDS = 6
LIMIT = 56 * 1024 * 1024


def vmem():
    return pl.BlockSpec(memory_space=pltpu.VMEM)


def smem():
    return pl.BlockSpec(memory_space=pltpu.SMEM)


def iota(shape, axis):
    return lax.broadcasted_iota(I32, shape, axis)


def one_hot(codes, shape, axis):
    index = iota(shape, axis).astype(jnp.int16)
    return jnp.where(codes.astype(jnp.int16) == index, jnp.ones(shape, BF16), jnp.zeros(shape, BF16))


def dot(a, b):
    return jnp.dot(a, b, preferred_element_type=F32)


def dot_lanes(a, b):
    return lax.dot_general(a, b, (((1,), (1,)), ((), ())), preferred_element_type=F32)


def split3(value):
    high = value.astype(BF16)
    rest = value - high.astype(F32)
    mid = rest.astype(BF16)
    return high, mid, (rest - mid.astype(F32)).astype(BF16)


def flat_lanes(array):
    n, k = array.shape
    per = 128 // k
    spread = jnp.concatenate([array] * per, axis=1)
    keep = iota((n, 128), 0) % per == iota((n, 128), 1) // k
    rows = jnp.sum(jnp.where(keep, spread, 0.0).reshape(n // per, per, 128), axis=1)
    return jnp.concatenate([rows[i : i + 1, :] for i in range(n // per)], axis=1)


def adagrad(values, accum_state, row_grads):
    renewed = accum_state + jnp.mean(row_grads * row_grads, axis=1, keepdims=True)
    return values - RATE * row_grads * lax.rsqrt(renewed), renewed


def column_of(scalars, rows, lanes, dtype):
    row = iota((rows, lanes), 0)
    out = jnp.zeros((rows, lanes), dtype)
    for i in range(rows):
        out = jnp.where(row == i, scalars(i), out)
    return out


def lanes_to_column(row):
    n = row.shape[1]
    return jnp.broadcast_to(row, (8, n)).T[:, :1]


def column_to_lanes(column):
    n = column.shape[0]
    return jnp.broadcast_to(column, (n, 128)).T[:1, :]


def wait_bytes(ref, sem):
    pltpu.make_async_copy(ref, ref, sem).wait()


def greet(axes):
    barrier = pltpu.get_barrier_semaphore()
    total = 0
    for axis in axes:
        n = lax.axis_size(axis)
        me = lax.axis_index(axis)

        def tell(o, carry, axis=axis, n=n, me=me):
            peer = lax.rem(me + o, n)
            pl.semaphore_signal(barrier, inc=1, device_id={axis: peer}, device_id_type=MESH)
            return carry

        lax.fori_loop(1, n, tell, 0)
        total += n - 1
    return barrier, total


def send_blocks(axis, src, dst, rows, per_peer, send_sem, recv_sem):
    n = lax.axis_size(axis)
    me = lax.axis_index(axis)

    def send(o, carry):
        peer = lax.rem(me + o, n)
        start = pl.multiple_of(peer * rows, rows) if per_peer else 0
        pltpu.make_async_remote_copy(
            src_ref=src.at[pl.ds(start, rows)],
            dst_ref=dst.at[pl.ds(pl.multiple_of(me * rows, rows), rows)],
            send_sem=send_sem,
            recv_sem=recv_sem,
            device_id={axis: peer},
            device_id_type=MESH,
        ).start()
        return carry

    lax.fori_loop(1, n, send, 0)


def own_block(axis, src, dst, rows, per_peer):
    me = lax.axis_index(axis)
    here = pl.ds(pl.multiple_of(me * rows, rows), rows)
    dst[here, :] = src[here, :] if per_peer else src[...]


Y = 8


def remote(src, dst, sems, peer):
    pltpu.make_async_remote_copy(
        src_ref=src, dst_ref=dst, send_sem=sems[0], recv_sem=sems[1], device_id={"table": peer}, device_id_type=MESH
    ).start()


def block_of(index, chips):
    return lax.rem(index, 2) * chips + index // 2


def some_rows(first, count, rows):
    return pl.ds(pl.multiple_of(first * rows, rows), count * rows)


def scatter_by_core(src, dst, rows, sems):
    n = lax.axis_size("table")
    me = lax.axis_index("table")
    here = some_rows(block_of(me, n // 2), 1, rows)

    def send(o, carry):
        peer = lax.rem(me + o, n)
        remote(src.at[some_rows(block_of(peer, n // 2), 1, rows)], dst.at[here], sems, peer)
        return carry

    lax.fori_loop(1, n, send, 0)
    dst[here, :] = src[here, :]


def gather_same_core(src, dst, rows, sems):
    n = lax.axis_size("table")
    me = lax.axis_index("table")
    chips = n // 2
    core, chip = lax.rem(me, 2), me // 2
    here = some_rows(block_of(me, chips), 1, rows)

    def send(o, carry):
        remote(src, dst.at[here], sems, lax.rem(chip + o, chips) * 2 + core)
        return carry

    lax.fori_loop(1, chips, send, 0)
    dst[here, :] = src[...]


def gather_other_core(dst, rows, sems):
    chips = lax.axis_size("table") // 2
    me = lax.axis_index("table")
    core = lax.rem(me, 2)
    half = some_rows(core * chips, chips, rows)
    remote(dst.at[half], dst.at[half], sems, me + 1 - 2 * core)


def gather_along_y(src, dst, rows, sems):
    n = lax.axis_size("table")
    me = lax.axis_index("table")
    core, chip = lax.rem(me, 2), me // 2
    here = some_rows(block_of(me, n // 2), 1, rows)
    for o in range(1, Y):
        peer = (chip // Y * Y + lax.rem(lax.rem(chip, Y) + o, Y)) * 2 + core
        remote(src, dst.at[here], sems, peer)
    dst[here, :] = src[...]


def gather_along_x(dst, rows, sems):
    n = lax.axis_size("table")
    me = lax.axis_index("table")
    chips = n // 2
    core, chip = lax.rem(me, 2), me // 2
    line = some_rows(core * chips + chip // Y * Y, Y, rows)
    for o in range(1, chips // Y):
        remote(dst.at[line], dst.at[line], sems, lax.rem(chip + o * Y, chips) * 2 + core)


def core_major(columns):
    n = columns.shape[1]
    at = iota((n, n), 1)
    order = iota((n, n), 0) == lax.rem(at, n // 2) * 2 + at // (n // 2)
    order = jnp.where(order, 1.0, 0.0).astype(BF16)
    high, low = columns >> 5, columns & 31
    return dot(high.astype(BF16), order) * 32.0 + dot(low.astype(BF16), order)


def step_kernel(
    promote_rows,
    demote_rows,
    demote_slots,
    cold_state_scalars,
    hot_state_scalars,
    lookups,
    labels,
    replica,
    hot_state,
    cold_table,
    cold_state,
    w_hbm,
    w_head,
    requests,
    tile_counts,
    promote_slots,
    logits,
    replica_next,
    hot_state_next,
    cold_next,
    cold_state_next,
    w_hidden,
    w_flipped,
    wanted_rows,
    served,
    fetched,
    base_own,
    base,
    demote_base,
    demote_bases,
    demote_grad,
    demote_grads,
    table,
    rows,
    cold_send,
    hot_send,
    cold_back,
    hot_back,
    local,
    local_send,
    promo_own,
    hot_own,
    cold_parts,
    promo_parts,
    cold_own,
    promo_sum,
    hot_grad,
    promo_grad,
    cold_grad,
    pick,
    start,
    total,
    w_sem,
    send_sem,
    recv_sem,
):
    n, groups = lax.axis_size("table"), lax.axis_size("dp")
    me, group = lax.axis_index("table"), lax.axis_index("dp")
    fields, batch = lookups.shape
    slots, width = replica.shape
    own = cold_table.shape[0]
    cap, pad = requests.shape[2], demote_slots.shape[1]
    share = own // groups
    half = table.shape[1]
    blocks = slots // half
    table_got = pl.ds(0, (n - 1) * cap)
    dp_got = groups - 1
    cells = base_own.shape[0]
    chips = n // 2
    sem = [(send_sem.at[i], recv_sem.at[i]) for i in range(send_sem.shape[0])]

    load = pltpu.make_async_copy(w_hbm, w_hidden, w_sem)
    load.start()
    barrier, greeted = greet(("table", "dp"))

    wanted = requests[group, 0]
    for j in range(n):
        wanted_rows[j * cap : (j + 1) * cap, :] = one_hot(wanted[:, j : j + 1], (cap, own), 1)
    served[...] = dot(wanted_rows[...], cold_table[...].astype(BF16)).astype(BF16)
    pl.semaphore_wait(barrier, greeted)
    send_blocks("table", served, fetched, cap, True, send_sem.at[0], recv_sem.at[0])
    own_block("table", served, fetched, cap, True)
    for i in range(pad):
        demote_base[i : i + 1, :] = replica[pl.ds(demote_slots[0, i], 1), :]
    demote_base[pad : 2 * pad, :] = column_of(lambda i: hot_state_scalars[0, demote_slots[0, i]], pad, width, F32)
    send_blocks("dp", demote_base, demote_bases, 2 * pad, False, send_sem.at[2], recv_sem.at[2])
    own_block("dp", demote_base, demote_bases, 2 * pad, False)

    for q in range(blocks):
        table[q * width : (q + 1) * width, :] = replica[q * half : (q + 1) * half, :].T.astype(BF16)
    def field(f):
        return pl.ds(pl.multiple_of(f * width, width), width)

    def by_fields(count, step):
        def some(k, carry):
            step([k * count + i for i in range(count)])
            return carry

        lax.fori_loop(0, fields // count, some, 0)
        if fields % count:
            step(list(range(fields - fields % count, fields)))

    def hot_entry(f):
        code = lookups[pl.ds(f, 1), :]
        found = dot(table[...], one_hot(code & (half - 1), (half, batch), 0))
        block = code >> (half.bit_length() - 1)
        entry = jnp.where(block == 0, found[:width, :], 0.0)
        for q in range(1, blocks):
            entry = jnp.where(block == q, found[q * width : (q + 1) * width, :], entry)
        rows[field(f), :] = entry.astype(BF16)

    by_fields(GATHER_FIELDS, lambda some: [hot_entry(f) for f in some])
    load.wait()

    def flip(f, carry):
        w_flipped[:, field(f)] = w_hidden[field(f), :].T
        return carry

    lax.fori_loop(0, fields, flip, 0)
    head = jnp.broadcast_to(w_head[...].astype(F32).reshape(1, -1), (width, w_head.shape[0])).T
    for i in range(pad):
        base_own[i : i + 1, :] = cold_table[pl.ds(promote_rows[0, i], 1), :]
    place = iota((8, width), 1)
    state = jnp.zeros((8, width), F32)
    for i in range(pad):
        state = jnp.where(place == i, cold_state_scalars[promote_rows[0, i]], state)
    base_own[pad:cells, :] = state

    wait_bytes(fetched.at[table_got], recv_sem.at[0])
    gather_along_y(base_own, base, cells, sem[1])
    for q in range(blocks):
        table[q * width : (q + 1) * width, :] = fetched[q * half : (q + 1) * half, :].astype(F32).T.astype(BF16)

    def cold_entry(f):
        code = lookups[pl.ds(f, 1), :]
        found = dot(table[...], one_hot(code & (half - 1), (half, batch), 0))
        block = code >> (half.bit_length() - 1)
        entry = rows[field(f), :].astype(F32)
        for q in range(blocks):
            entry = jnp.where(block == blocks + q, found[q * width : (q + 1) * width, :], entry)
        rows[field(f), :] = entry.astype(BF16)

    by_fields(GATHER_FIELDS, lambda some: [cold_entry(f) for f in some])

    wait_bytes(base.at[pl.ds(0, (Y - 1) * cells)], recv_sem.at[1])
    gather_along_x(base, cells, sem[11])

    hidden = dot(w_flipped[...], rows[...])
    sig = jax.nn.sigmoid(hidden)
    heads = jnp.concatenate([head] * (batch // width), axis=1)
    logit = jnp.sum(hidden * sig * heads, axis=0, keepdims=True)
    logits[...] = logit
    residue = jax.nn.sigmoid(logit) - labels[...].astype(F32)
    slope = sig * (1.0 + hidden * (1.0 - sig))
    hidden_grad = (residue * heads * slope).astype(BF16)
    rows[...] = dot(w_hidden[...], hidden_grad).astype(BF16)

    def summed(first, out):
        total[...] = jnp.zeros_like(total)

        def add(some):
            picks, grads = [], []
            for f in some:
                code = lookups[pl.ds(f, 1), :]
                block = code >> (half.bit_length() - 1)
                grad = rows[field(f), :]
                keep = [jnp.where(block == first + q, 1.0, 0.0).astype(BF16) for q in range(blocks)]
                grads.append(jnp.concatenate([grad * mask for mask in keep], axis=0))
                picks.append(one_hot(code & (half - 1), (half, batch), 0))
            total[...] += dot_lanes(jnp.concatenate(picks, axis=1), jnp.concatenate(grads, axis=1))

        by_fields(SUM_FIELDS, add)
        for q in range(blocks):
            out[q * half : (q + 1) * half, :] = total[:, q * width : (q + 1) * width].astype(BF16)

    wait_bytes(base.at[pl.ds(0, (chips - Y) * cells)], recv_sem.at[11])
    gather_other_core(base, cells, sem[12])
    summed(blocks, cold_send)
    send_blocks("table", cold_send, cold_back, cap, True, send_sem.at[3], recv_sem.at[3])
    own_block("table", cold_send, cold_back, cap, True)
    summed(0, hot_send)
    scatter_by_core(hot_send, hot_back, cap, sem[4])

    to_rows = one_hot(flat_lanes(wanted.astype(F32).T).astype(I32), (own, n * cap), 0)
    demote_hot = one_hot(column_of(lambda i: demote_slots[0, i], pad, slots, I32), (pad, slots), 1)

    wait_bytes(cold_back.at[table_got], recv_sem.at[3])
    local[...] = dot(to_rows, cold_back[...])
    promo_own[...] = jnp.concatenate([local[pl.ds(promote_rows[0, i], 1), :] for i in range(pad)], axis=0).astype(BF16)
    local_send[...] = local[...].astype(BF16)
    send_blocks("dp", promo_own, promo_parts, pad, False, send_sem.at[5], recv_sem.at[5])
    send_blocks("dp", local_send, cold_parts, share, True, send_sem.at[6], recv_sem.at[6])
    own_block("dp", promo_own, promo_parts, pad, False)
    own_block("dp", local_send, cold_parts, share, True)
    wait_bytes(hot_back.at[table_got], recv_sem.at[4])
    hot_own[...] = jnp.sum(hot_back[...].astype(F32).reshape(n, cap, width), axis=0).astype(BF16)
    gather_same_core(hot_own, hot_grad, cap, sem[7])
    wait_bytes(promo_parts.at[pl.ds(0, dp_got * pad)], recv_sem.at[5])
    promo_sum[...] = jnp.sum(promo_parts[...].astype(F32).reshape(groups, pad, width), axis=0).astype(BF16)
    gather_same_core(promo_sum, promo_grad, pad, sem[8])
    wait_bytes(cold_parts.at[pl.ds(0, dp_got * share)], recv_sem.at[6])
    cold_own[...] = jnp.sum(cold_parts[...].astype(F32).reshape(groups, share, width), axis=0).astype(BF16)
    send_blocks("dp", cold_own, cold_grad, share, False, send_sem.at[9], recv_sem.at[9])
    own_block("dp", cold_own, cold_grad, share, False)
    counts = tile_counts[...]
    live = iota((pad, n), 0) < counts[1:2, :] * TILE
    targets = flat_lanes(core_major(jnp.where(live, promote_slots[...], slots)).T).astype(I32)
    pick[...] = one_hot(targets, (slots, n * pad), 0)
    wait_bytes(base.at[pl.ds(0, chips * cells)], recv_sem.at[12])
    bases = base[...].reshape(n, cells, width)
    chosen = dot(pick[...], jnp.concatenate(split3(bases[:, :pad].reshape(n * pad, width)), axis=1))
    picked = (chosen[:, :width] + chosen[:, width : 2 * width]) + chosen[:, 2 * width :]
    state_lanes = flat_lanes(bases[:, pad, :pad])
    pieces = [piece.astype(F32) for piece in split3(state_lanes)]
    side_rows = jnp.concatenate(pieces + [jnp.ones_like(state_lanes)] + [jnp.zeros_like(state_lanes)] * 4, axis=0)
    side = dot_lanes(pick[...], side_rows.astype(BF16))
    promoted = side[:, 3:4] > 0.0
    start[...] = jnp.where(promoted, picked, replica[...])
    start_state = jnp.where(promoted, (side[:, 0:1] + side[:, 1:2]) + side[:, 2:3], lanes_to_column(hot_state[...]))
    cold_column = lanes_to_column(cold_state[...])
    core_got = pl.ds(0, (chips - 1) * cap)
    half_got = pl.ds(0, chips * cap)
    wait_bytes(hot_grad.at[core_got], recv_sem.at[7])
    gather_other_core(hot_grad, cap, sem[13])
    wait_bytes(hot_grad.at[half_got], recv_sem.at[13])
    demote_grad[...] = dot(demote_hot, hot_grad[...]).astype(BF16)
    send_blocks("dp", demote_grad, demote_grads, pad, False, send_sem.at[10], recv_sem.at[10])
    own_block("dp", demote_grad, demote_grads, pad, False)
    wait_bytes(promo_grad.at[core_got], recv_sem.at[8])
    gather_other_core(promo_grad, pad, sem[14])
    wait_bytes(cold_grad.at[pl.ds(0, dp_got * share)], recv_sem.at[9])
    values, renewed = adagrad(cold_table[...], cold_column, cold_grad[...].astype(F32))
    wait_bytes(promo_grad.at[half_got], recv_sem.at[14])
    grad = jnp.where(promoted, dot(pick[...], promo_grad[...]), hot_grad[...].astype(F32))
    hot_values, hot_renewed = adagrad(start[...], start_state, grad)
    replica_next[...] = hot_values
    hot_state_next[...] = column_to_lanes(hot_renewed)
    wait_bytes(demote_bases.at[pl.ds(0, dp_got * 2 * pad)], recv_sem.at[2])
    wait_bytes(demote_grads.at[pl.ds(0, dp_got * pad)], recv_sem.at[10])
    mean = jnp.zeros((2 * pad, width), F32)
    for g in range(groups):
        old, old_state = demote_bases[2 * pad * g : 2 * pad * g + pad, :], demote_bases[2 * pad * g + pad : 2 * pad * (g + 1), :]
        new, new_state = adagrad(old, old_state, demote_grads[pad * g : pad * (g + 1), :].astype(F32))
        mean += jnp.concatenate([new, new_state], axis=0)
    mean = mean / groups
    renewed = jnp.broadcast_to(renewed, (own, width))
    count = jnp.sum(jnp.where(iota((1, n), 1) == me, counts[0:1, :], 0), axis=1, keepdims=True) * TILE
    row = iota((own, width), 0)
    for i in range(pad):
        here = (row == demote_rows[0, i]) & (i < count)
        values = jnp.where(here, mean[i : i + 1, :], values)
        renewed = jnp.where(here, mean[pad + i : pad + i + 1, :], renewed)
    cold_next[...] = values
    cold_state_next[...] = renewed.T[:1, :]

    for i, sent in enumerate(
        (
            fetched.at[table_got],
            base.at[pl.ds(0, (Y - 1) * cells)],
            demote_bases.at[pl.ds(0, dp_got * 2 * pad)],
            cold_back.at[table_got],
            hot_back.at[table_got],
            promo_parts.at[pl.ds(0, dp_got * pad)],
            cold_parts.at[pl.ds(0, dp_got * share)],
            hot_grad.at[core_got],
            promo_grad.at[core_got],
            cold_grad.at[pl.ds(0, dp_got * share)],
            demote_grads.at[pl.ds(0, dp_got * pad)],
            base.at[pl.ds(0, (chips - Y) * cells)],
            base.at[pl.ds(0, chips * cells)],
            hot_grad.at[half_got],
            promo_grad.at[half_got],
        )
    ):
        wait_bytes(sent, send_sem.at[i])


def finish_kernel(*refs):
    count = len(refs) // 2
    for i in range(count):
        refs[count + i][...] = refs[i][...]


def body(
    lookups,
    labels,
    replica,
    hot_state,
    cold_table,
    cold_state,
    w_hidden,
    w_head,
    requests,
    tile_counts,
    demote_slots,
    demote_rows,
    promote_slots,
    promote_rows,
):
    batch, fields = lookups.shape
    slots, width = replica.shape[1:]
    own = cold_table.shape[0]
    groups, n = lax.axis_size("dp"), lax.axis_size("table")
    cap = requests.shape[3]
    pad = demote_slots.shape[1]
    inputs, units = w_hidden.shape
    dma = pltpu.SemaphoreType.DMA
    shape = jax.ShapeDtypeStruct
    results = (
        shape((1, batch), F32),
        shape((slots, width), F32),
        shape((1, slots), F32),
        shape((own, width), F32),
        shape((1, own), F32),
    )
    found = pl.pallas_call(
        step_kernel,
        out_shape=results,
        in_specs=[smem()] * 5 + [vmem()] * 6 + [pl.BlockSpec(memory_space=pl.ANY)] + [vmem()] * 4,
        out_specs=(vmem(),) * 5,
        scratch_shapes=[
            pltpu.VMEM((inputs, units), BF16),
            pltpu.VMEM((units, inputs), BF16),
            pltpu.VMEM((n * cap, own), BF16),
            pltpu.VMEM((n * cap, width), BF16),
            pltpu.VMEM((n * cap, width), BF16),
            pltpu.VMEM((pad + 8, width), F32),
            pltpu.VMEM((n * (pad + 8), width), F32),
            pltpu.VMEM((2 * pad, width), F32),
            pltpu.VMEM((groups * 2 * pad, width), F32),
            pltpu.VMEM((pad, width), BF16),
            pltpu.VMEM((groups * pad, width), BF16),
            pltpu.VMEM((2 * width, 512), BF16),
            pltpu.VMEM((inputs, batch), BF16),
            pltpu.VMEM((n * cap, width), BF16),
            pltpu.VMEM((slots, width), BF16),
            pltpu.VMEM((n * cap, width), BF16),
            pltpu.VMEM((slots, width), BF16),
            pltpu.VMEM((own, width), F32),
            pltpu.VMEM((own, width), BF16),
            pltpu.VMEM((pad, width), BF16),
            pltpu.VMEM((slots // n, width), BF16),
            pltpu.VMEM((own, width), BF16),
            pltpu.VMEM((groups * pad, width), BF16),
            pltpu.VMEM((own // groups, width), BF16),
            pltpu.VMEM((pad, width), BF16),
            pltpu.VMEM((slots, width), BF16),
            pltpu.VMEM((n * pad, width), BF16),
            pltpu.VMEM((own, width), BF16),
            pltpu.VMEM((slots, n * pad), BF16),
            pltpu.VMEM((slots, width), F32),
            pltpu.VMEM((512, 2 * width), F32),
            dma,
            dma((15,)),
            dma((15,)),
        ],
        compiler_params=pltpu.CompilerParams(collective_id=0, has_side_effects=True, vmem_limit_bytes=LIMIT),
        name="step",
    )(
        promote_rows,
        demote_rows,
        demote_slots,
        cold_state,
        hot_state,
        lookups.T,
        labels.reshape(1, batch),
        replica[0],
        hot_state,
        cold_table,
        cold_state.reshape(1, own),
        w_hidden,
        w_head,
        requests.transpose(0, 1, 3, 2),
        tile_counts.T,
        promote_slots.T,
    )
    logits, replica_next, hot_state_next, cold_next, cold_state_next = pl.pallas_call(
        finish_kernel,
        out_shape=results,
        in_specs=[vmem()] * 5,
        out_specs=[vmem()] * 5,
        compiler_params=pltpu.CompilerParams(vmem_limit_bytes=LIMIT),
        name="finish",
    )(*found)
    return (logits[0], replica_next[None], hot_state_next, cold_next, cold_state_next[0])


def solution(mesh):
    return jax.shard_map(
        body,
        mesh=mesh,
        in_specs=(
            P(("dp", "table"), None),
            P(("dp", "table")),
            P("dp", None, None),
            P("dp", None),
            P("table", None),
            P("table"),
            P(),
            P(),
            P(None, "table", None, None),
            P(),
            P("table", None),
            P("table", None),
            P(),
            P("table", None),
        ),
        out_specs=(
            P(("dp", "table")),
            P("dp", None, None),
            P("dp", None),
            P("table", None),
            P("table"),
        ),
        check_vma=False,
    )
```
